32 devices in a mesh: groups: 2 (over y), replica: 16 (over z, x, core).
Axes of the slice: x: 2, y: 2, z: 4, core: 2. Of those that a mesh axis runs over, the one named last changes fastest.
Arguments:
- queries: bfloat16 [64, 4, 4096], P(('groups', 'replica')), parts along dimension 0, may hold values from -4 to 4
- keys: bfloat16 [64, 4, 4096], P(('groups', 'replica')), parts along dimension 0, may hold values from -4 to 4
- values: bfloat16 [64, 4, 4096], P(('groups', 'replica')), parts along dimension 0, may hold values from -6 to 6
- gate_input: bfloat16 [64, 4, 4096], P(('groups', 'replica')), parts along dimension 0, may hold values from -6 to 6
- decay_rate: float32 [32], replicated, may hold values from 0.05 to 1.5
- norm_gain: float32 [4096], replicated, may hold values from 0.1 to 1.9
- out_weight: bfloat16 [4096, 3072], P('replica'), may hold values from -0.09375 to 0.09375
- prompt_states: bfloat16 [8, 4096, 128], P('groups', 'replica'), parts along dimension 0, may hold values from -4 to 4
- group_sizes: int32 [8], P('groups'), parts along dimension 0, may hold values from 1 to 16, 32 in all
Outputs:
- mixed: bfloat16 [64, 4, 3072], P(('groups', 'replica')), parts along dimension 0
The draws below stay inside these ranges and needn't reach their ends.
There are 2 independent parts, one for each index of `groups`. The reference program is written for one: setup_inputs(seed, part) draws one part's arguments, and reference() takes and returns one part's arrays. A program takes and returns all parts, laid end to end along the dimension named above; an argument that names none is the same for every part. Nothing has to cross between parts.
Inputs may be any that keep to these rules, and one draw needn't show every extreme that they name: `group_sizes`: the group sizes sum to 32, and the largest is exactly 16.
All inputs are finite; a program needn't handle non-finite values.
Results may differ from the reference program's by a relative error of at most 0.005.
Values may be sent and summed in bfloat16 or wider, within the bound.
A program may use at most 64 MiB of HBM per device.

```python
import math
import jax
import jax.numpy as jnp
import numpy as np
from jax import lax

D = 3072
HEADS = 32
HD = 128
STEPS = 4
ROWS = 32
PROMPTS = 4
MOST = 16


def steps_of(rng, shape, cuts, low, top_value):
    level = 1.0
    for axis_at, shards_of in cuts:
        heights = jax.random.uniform(jax.random.fold_in(jax.random.fold_in(rng, 6), axis_at), (shards_of,), jnp.float32, low / len(cuts), top_value / len(cuts))
        level = level * jnp.repeat(jnp.exp(heights), shape[axis_at] // shards_of).reshape((-1,) + (1,) * (len(shape) - 1 - axis_at))
    return level


def split_up(number_of, total, bound, slope):
    weights = [(1 << 20) // math.isqrt(grade ** slope) + 1 for grade in range(2, number_of + 1)]
    spare, holding = total - bound - (number_of - 1), [1] * (number_of - 1)
    while spare > 0:
        free = [i for i in range(number_of - 1) if holding[i] < bound]
        pool, remaining = sum([weights[i] for i in free]), spare
        for i in free:
            extra = min(bound - holding[i], max(1, remaining * weights[i] // pool), spare)
            holding[i] = holding[i] + extra
            spare = spare - extra
    return np.array([bound] + holding)


def ragged(key, number_of, total, reach, slope):
    if number_of == 2:
        one = jax.random.randint(key, (), max(1, total - reach), min(reach, total - 1) + 1)
        return jnp.stack([one, total - one])
    lengths = jnp.asarray(split_up(number_of, total, reach, slope), jnp.int32)
    couples = (number_of - 1) // 2
    donor, taker = lengths[1:1 + 2 * couples:2], lengths[2:2 + 2 * couples:2]
    room = jnp.minimum(donor - 1, reach - taker)
    passed = jax.random.randint(jax.random.fold_in(key, 1), (couples,), 0, 1 << 20) % (room + 1)
    lengths = lengths.at[1:1 + 2 * couples:2].set(donor - passed).at[2:2 + 2 * couples:2].set(taker + passed)
    return lengths[jax.random.permutation(jax.random.fold_in(key, 2), number_of)]


def noise(stream_key, dims, scale, limit, cuts=(), kind=jnp.bfloat16):
    array = jax.random.normal(stream_key, dims, jnp.float32) * scale
    if len(cuts) > 0:
        array = steps_of(stream_key, dims, cuts, -0.22, 0.18) * array
    return jnp.clip(array, min=-limit, max=limit).astype(kind)


def setup_inputs(seed: int = 0, part: int = 0) -> dict:
    arg_keys = jax.random.split(jax.random.key(seed), 10)
    part_splits = jax.random.split(jax.random.fold_in(arg_keys[9], part), 10)
    return {
        "queries": noise(part_splits[0], (ROWS, STEPS, HEADS * HD), 0.3, 4.0, ((0, 16),)),
        "keys": noise(part_splits[1], (ROWS, STEPS, HEADS * HD), 0.3, 4.0, ((0, 16),)),
        "values": noise(part_splits[2], (ROWS, STEPS, HEADS * HD), 1.0, 6.0, ((0, 16),)),
        "gate_input": noise(part_splits[3], (ROWS, STEPS, HEADS * HD), 1.0, 6.0, ((0, 16),)),
        "decay_rate": jnp.clip(jnp.exp(jax.random.uniform(arg_keys[4], (HEADS,), jnp.float32, math.log(0.05), math.log(1.5))), 0.05, 1.5),
        "norm_gain": jnp.clip(1.0 + 0.18 * jax.random.normal(arg_keys[5], (HEADS * HD,), jnp.float32), 0.1, 1.9),
        "out_weight": noise(arg_keys[6], (HEADS * HD, D), (HEADS * HD) ** -0.5, 0.09375, ((0, 16),)),
        "prompt_states": noise(part_splits[7], (PROMPTS, HEADS * HD, HD), 0.3, 4.0, ((1, 16),)),
        "group_sizes": ragged(part_splits[8], PROMPTS, ROWS, MOST, 2).astype(jnp.int32),
    }


def reference(queries, keys, values, gate_input, decay_rate, norm_gain, out_weight, prompt_states, group_sizes):
    rows_total, steps_count, features = queries.shape
    head_size = prompt_states.shape[2]
    head_count = features // head_size
    ends = jnp.cumsum(group_sizes).astype(jnp.int32)
    row_ids = jnp.arange(rows_total, dtype=jnp.int32)
    owners = lax.optimization_barrier(jnp.sum((row_ids[:, None] >= ends[None, :]).astype(jnp.int32), axis=1)).astype(jnp.int32)

    def read_one(pair):
        query_row, prompt_id = pair
        state = lax.dynamic_index_in_dim(prompt_states, prompt_id, 0, keepdims=False)
        state = state.astype(jnp.float32).reshape(head_count, head_size, head_size)
        query_four = query_row.astype(jnp.float32).reshape(steps_count, head_count, head_size)
        return jnp.einsum('thd,hde->the', query_four, state, precision=lax.Precision.HIGHEST)
    prompt_read = lax.map(read_one, (queries, owners))
    q_four = queries.astype(jnp.float32).reshape(rows_total, steps_count, head_count, head_size)
    k_four = keys.astype(jnp.float32).reshape(rows_total, steps_count, head_count, head_size)
    v_four = values.astype(jnp.float32).reshape(rows_total, steps_count, head_count, head_size)
    times = jnp.arange(1, steps_count + 1).astype(jnp.float32)
    lead = jnp.exp(-times[:, None] * decay_rate[None, :])
    gap = times[:, None] - times[None, :]
    weights_mix = jnp.where(gap[None] >= 0.0, jnp.exp(-jnp.maximum(gap, 0.0)[None] * decay_rate[:, None, None]), 0.0)
    scores = jnp.einsum('rthd,rshd->rhts', q_four, k_four, precision=lax.Precision.HIGHEST)
    recent = jnp.einsum('rhts,rshe->rthe', scores * weights_mix[None], v_four, precision=lax.Precision.HIGHEST)
    attention = lead[None, :, :, None] * prompt_read + recent
    attention = attention.reshape(rows_total, steps_count, features)
    mean_square = lax.optimization_barrier(jnp.mean(attention * attention, axis=-1, keepdims=True))
    gate = jax.nn.sigmoid(gate_input.astype(jnp.float32))
    hidden = (attention * lax.rsqrt(mean_square + 1e-06) * norm_gain * gate).astype(jnp.bfloat16)
    mixed = jnp.dot(hidden.reshape(rows_total * steps_count, features), out_weight, preferred_element_type=jnp.float32)
    return mixed.astype(jnp.bfloat16).reshape(rows_total, steps_count, out_weight.shape[1])
```

```python
import functools

import jax
import jax.numpy as jnp
from jax import lax
from jax.experimental import pallas as pl
from jax.experimental.pallas import tpu as pltpu
from jax.sharding import PartitionSpec as P

MESH = pl.DeviceIdType.MESH
F32 = jnp.float32
BF16 = jnp.bfloat16


def kernel(
    chips,
    q_ref, k_ref, v_ref, g_ref, decay_ref, gain_ref, w_hbm, st_hbm, gs_ref,
    out_ref,
    stage, sbuf, rbuf, w_buf, st_buf, pbuf, precv, own, ss_send, ss_recv,
    local_sem, pair_send, pair_recv, x_send, x_recv, p_send, p_recv, s_send, s_recv,
):
    rows_local, steps, features = q_ref.shape
    tokens_local = rows_local * steps
    prompts, share, hd = st_hbm.shape
    wide = 2 * share
    heads_device = share // hd
    half = w_hbm.shape[1] // 2
    tokens = chips * tokens_local
    me = lax.axis_index("replica")
    chip = me // 2
    core = lax.rem(me, 2)
    partner = chip * 2 + 1 - core

    def peer(chip_index):
        return {"replica": lax.rem(chip_index + chips, chips) * 2 + core}

    w_own = pltpu.make_async_copy(w_hbm, w_buf.at[core], local_sem.at[0])
    st_own = pltpu.make_async_copy(st_hbm, st_buf.at[core], local_sem.at[1])
    st_own.start()
    w_own.start()

    barrier = pltpu.get_barrier_semaphore()
    pl.semaphore_signal(barrier, inc=1, device_id={"replica": partner}, device_id_type=MESH)
    for o in range(1, chips):
        pl.semaphore_signal(barrier, inc=1, device_id=peer(chip + o), device_id_type=MESH)

    for kind, ref in enumerate((q_ref, k_ref, v_ref, g_ref)):
        for r in range(rows_local):
            at = kind * tokens_local + r * steps
            stage[at:at + steps, :] = ref[r].astype(F32)
    for o in range(chips):
        off = pl.multiple_of(lax.rem(chip + o, chips) * wide, wide)
        block = stage[:, pl.ds(off, wide)].astype(BF16)
        if o == 0:
            rbuf[0] = block
        else:
            sbuf[o] = block

    pl.semaphore_wait(barrier, chips)

    x_copies = []
    for o in range(1, chips):
        copy = pltpu.make_async_remote_copy(
            src_ref=sbuf.at[o], dst_ref=rbuf.at[o], send_sem=x_send.at[o], recv_sem=x_recv.at[o],
            device_id=peer(chip + o), device_id_type=MESH,
        )
        copy.start()
        x_copies.append(copy)
    st_pair = pltpu.make_async_remote_copy(
        src_ref=st_hbm, dst_ref=st_buf.at[core], send_sem=pair_send.at[0], recv_sem=pair_recv.at[0],
        device_id={"replica": partner}, device_id_type=MESH,
    )
    st_pair.start()
    w_pair = pltpu.make_async_remote_copy(
        src_ref=w_hbm, dst_ref=w_buf.at[core], send_sem=pair_send.at[1], recv_sem=pair_recv.at[1],
        device_id={"replica": partner}, device_id_type=MESH,
    )
    w_pair.start()

    token = lax.broadcasted_iota(jnp.int32, (tokens, 1), 0)
    source = lax.rem(chip - token // tokens_local + chips, chips)
    row = (source * 2 + core) * rows_local + lax.rem(token, tokens_local) // steps
    step = lax.rem(token, steps)
    lead_time = (step + 1).astype(F32)
    ti = lax.broadcasted_iota(jnp.int32, (tokens, tokens), 0)
    si = lax.broadcasted_iota(jnp.int32, (tokens, tokens), 1)
    live = (ti // steps == si // steps) & (si <= ti)
    gap = jnp.maximum(ti - si, 0).astype(F32)
    masks = []
    start = jnp.int32(0)
    for p in range(prompts):
        end = start + gs_ref[p]
        masks.append((row >= start) & (row < end))
        start = end

    st_own.wait()
    st_pair.wait()
    for copy in x_copies:
        copy.wait()

    us = []
    square = jnp.zeros((tokens, 1), F32)
    for h in range(2 * heads_device):
        head = chip * 2 * heads_device + h
        cols = slice(h * hd, (h + 1) * hd)
        block = rbuf[:, :, cols].astype(F32)
        q, k, v, g = (
            block[:, i * tokens_local:(i + 1) * tokens_local, :].reshape(tokens, hd) for i in range(4)
        )
        decay = decay_ref[head]
        read = jnp.zeros((tokens, hd), F32)
        keys_at = (h % heads_device) * hd
        for p in range(prompts):
            state = st_buf[h // heads_device, p, keys_at:keys_at + hd, :]
            read += jnp.dot(
                jnp.where(masks[p], q, 0.0).astype(BF16), state, preferred_element_type=F32
            )
        scores = lax.dot_general(
            q.astype(BF16), k.astype(BF16), (((1,), (1,)), ((), ())), preferred_element_type=F32
        )
        scores = scores * jnp.where(live, jnp.exp(-gap * decay), 0.0)
        high = scores.astype(BF16)
        low = (scores - high.astype(F32)).astype(BF16)
        vb = v.astype(BF16)
        recent = jnp.dot(high, vb, preferred_element_type=F32) + jnp.dot(
            low, vb, preferred_element_type=F32
        )
        attention = jnp.exp(-lead_time * decay) * read + recent
        square += jnp.sum(attention * attention, axis=1, keepdims=True)
        gain = gain_ref[pl.ds(head, 1), :]
        us.append((attention * gain * jax.nn.sigmoid(g)).astype(BF16))

    ss_send[...] = jnp.broadcast_to(square, (tokens, 128)).reshape(chips, tokens_local, 128)
    s_copies = []
    for o in range(1, chips):
        copy = pltpu.make_async_remote_copy(
            src_ref=ss_send.at[o], dst_ref=ss_recv.at[o], send_sem=s_send.at[o], recv_sem=s_recv.at[o],
            device_id=peer(chip - o), device_id_type=MESH,
        )
        copy.start()
        s_copies.append(copy)

    u0 = jnp.concatenate(us[:heads_device], axis=1)
    u1 = jnp.concatenate(us[heads_device:], axis=1)
    w_own.wait()
    w_pair.wait()
    parts, tile = pbuf.shape[0], pbuf.shape[3]
    p_copies = []
    for c in range(parts):
        pieces = []
        for base in (0, half):
            at = slice(base + c * tile, base + (c + 1) * tile)
            y = jnp.dot(u0, w_buf[0, :, at], preferred_element_type=F32)
            y += jnp.dot(u1, w_buf[1, :, at], preferred_element_type=F32)
            pieces.append(y.reshape(chips, tokens_local, tile))
        both = jnp.concatenate(pieces, axis=1)
        own[c] = both[0]
        pbuf[c] = both.astype(BF16)
        for o in range(1, chips):
            copy = pltpu.make_async_remote_copy(
                src_ref=pbuf.at[c, o], dst_ref=precv.at[c, o],
                send_sem=p_send.at[c, o], recv_sem=p_recv.at[c, o],
                device_id=peer(chip - o), device_id_type=MESH,
            )
            copy.start()
            p_copies.append(copy)

    for copy in s_copies:
        copy.wait()
    total_square = ss_send[0]
    for o in range(1, chips):
        total_square += ss_recv[o]
    scale = lax.rsqrt(total_square / features + 1e-06)[:, 0:1]
    for c in range(parts):
        total = own[c]
        for o in range(1, chips):
            p_copies[c * (chips - 1) + o - 1].wait()
            total += precv[c, o].astype(F32)
        for i, base in enumerate((0, half)):
            result = total[i * tokens_local:(i + 1) * tokens_local, :] * scale
            at = slice(base + c * tile, base + (c + 1) * tile)
            for r in range(rows_local):
                out_ref[r, :, at] = result[r * steps:(r + 1) * steps, :].astype(BF16)


def fused(
    queries, keys, values, gate_input, decay_rate, norm_gain, out_weight, prompt_states, group_sizes
):
    chips = lax.axis_size("replica") // 2
    rows_local, steps, features = queries.shape
    prompts, share, hd = prompt_states.shape
    width = out_weight.shape[1]
    tokens_local = rows_local * steps
    parts = 2
    tile = width // 2 // parts
    vmem = pl.BlockSpec(memory_space=pltpu.VMEM)
    smem = pl.BlockSpec(memory_space=pltpu.SMEM)
    hbm = pl.BlockSpec(memory_space=pl.ANY)
    dma = pltpu.SemaphoreType.DMA
    return pl.pallas_call(
        functools.partial(kernel, chips),
        out_shape=jax.ShapeDtypeStruct((rows_local, steps, width), BF16),
        in_specs=[vmem, vmem, vmem, vmem, smem, vmem, hbm, hbm, smem],
        out_specs=vmem,
        scratch_shapes=[
            pltpu.VMEM((4 * tokens_local, features), F32),
            pltpu.VMEM((chips, 4 * tokens_local, 2 * share), BF16),
            pltpu.VMEM((chips, 4 * tokens_local, 2 * share), BF16),
            pltpu.VMEM((2, share, width), BF16),
            pltpu.VMEM((2, prompts, share, hd), BF16),
            pltpu.VMEM((parts, chips, 2 * tokens_local, tile), BF16),
            pltpu.VMEM((parts, chips, 2 * tokens_local, tile), BF16),
            pltpu.VMEM((parts, 2 * tokens_local, tile), F32),
            pltpu.VMEM((chips, tokens_local, 128), F32),
            pltpu.VMEM((chips, tokens_local, 128), F32),
            dma((2,)), dma((2,)), dma((2,)),
            dma((chips,)), dma((chips,)),
            dma((parts, chips)), dma((parts, chips)),
            dma((chips,)), dma((chips,)),
        ],
        compiler_params=pltpu.CompilerParams(
            collective_id=0, has_side_effects=True, vmem_limit_bytes=48 * 1024 * 1024
        ),
    )(
        queries, keys, values, gate_input, decay_rate, norm_gain.reshape(-1, hd),
        out_weight, prompt_states, group_sizes,
    )


def general(
    queries, keys, values, gate_input, decay_rate, norm_gain, out_weight, prompt_states, group_sizes
):
    replicas = lax.axis_size("replica")
    rows_local, steps_count, features = queries.shape
    head_size = prompt_states.shape[2]
    head_count = features // head_size
    share = prompt_states.shape[1]
    rows_total = rows_local * replicas
    ends = jnp.cumsum(group_sizes)
    row_ids = jnp.arange(rows_total, dtype=jnp.int32)
    owners = jnp.sum((row_ids[:, None] >= ends[None, :]).astype(jnp.int32), axis=1)
    q_four = queries.reshape(rows_local, steps_count, head_count, head_size)
    k_four = keys.reshape(rows_local, steps_count, head_count, head_size)
    v_four = values.astype(F32).reshape(rows_local, steps_count, head_count, head_size)
    piece = min(share, head_size)
    pieces_here = share // piece
    per_head = head_size // piece
    query_parts = queries.reshape(rows_local, steps_count, replicas, share)
    held_queries = lax.all_to_all(query_parts, "replica", split_axis=2, concat_axis=0, tiled=True)
    held_queries = held_queries.reshape(rows_total, steps_count, pieces_here, piece)
    held_states = jnp.take(prompt_states, owners, axis=0).reshape(
        rows_total, pieces_here, piece, head_size
    )
    partial_value = jnp.einsum(
        "rtcd,rcde->rtce", held_queries, held_states, preferred_element_type=F32
    )
    partial_value = partial_value.reshape(replicas, rows_local, steps_count, pieces_here, head_size)
    returned = lax.all_to_all(partial_value, "replica", split_axis=0, concat_axis=0, tiled=True)
    returned = jnp.moveaxis(returned, 0, 2)
    returned = returned.reshape(rows_local, steps_count, head_count, per_head, head_size)
    prompt_read = jnp.sum(returned, axis=3)
    times = jnp.arange(1, steps_count + 1).astype(F32)
    lead = jnp.exp(-times[:, None] * decay_rate[None, :])
    gap = times[:, None] - times[None, :]
    weights_mix = jnp.where(
        gap[None] >= 0.0, jnp.exp(-jnp.maximum(gap, 0.0)[None] * decay_rate[:, None, None]), 0.0
    )
    scores = jnp.einsum("rthd,rshd->rhts", q_four, k_four, preferred_element_type=F32)
    recent = jnp.einsum(
        "rhts,rshe->rthe", scores * weights_mix[None], v_four, precision=lax.Precision.HIGHEST
    )
    attention = lead[None, :, :, None] * prompt_read + recent
    attention = attention.reshape(rows_local, steps_count, features)
    mean_square = jnp.mean(attention * attention, axis=-1, keepdims=True)
    gate = jax.nn.sigmoid(gate_input.astype(F32))
    hidden = (attention * lax.rsqrt(mean_square + 1e-06) * norm_gain * gate).astype(BF16)
    hidden = hidden.reshape(rows_local * steps_count, features)
    columns_held = lax.all_to_all(hidden, "replica", split_axis=1, concat_axis=0, tiled=True)
    sums = jnp.dot(columns_held, out_weight, preferred_element_type=F32)
    sums = sums.reshape(replicas, rows_local * steps_count, out_weight.shape[1])
    sums = lax.all_to_all(sums, "replica", split_axis=0, concat_axis=0, tiled=True)
    mixed = jnp.sum(sums, axis=0)
    return mixed.astype(BF16).reshape(rows_local, steps_count, out_weight.shape[1])


def on_device(*args):
    prompt_states = args[7]
    if prompt_states.shape[1] % prompt_states.shape[2] == 0:
        return fused(*args)
    return general(*args)


def solution(mesh):
    rows = P(("groups", "replica"), None, None)
    in_specs = (
        rows, rows, rows, rows, P(), P(), P("replica", None), P("groups", "replica", None), P("groups"),
    )
    return jax.shard_map(
        on_device, mesh=mesh, in_specs=in_specs, out_specs=rows, check_vma=False
    )
```

```python
import functools

import jax
import jax.numpy as jnp
from jax import lax
from jax.experimental import pallas as pl
from jax.experimental.pallas import tpu as pltpu
from jax.sharding import PartitionSpec as P

MESH = pl.DeviceIdType.MESH
F32 = jnp.float32
BF16 = jnp.bfloat16


def kernel(
    chips,
    q_ref, k_ref, v_ref, g_ref, decay_ref, gain_ref, w_hbm, st_hbm, gs_ref,
    out_ref,
    stage, sbuf, rbuf, w_buf, st_buf, pbuf, precv, own, ss_send, ss_recv,
    local_sem, pair_send, pair_recv, x_send, x_recv, p_send, p_recv, s_send, s_recv,
):
    rows_local, steps, features = q_ref.shape
    tokens_local = rows_local * steps
    prompts, share, hd = st_hbm.shape
    wide = 2 * share
    heads_device = share // hd
    half = w_hbm.shape[1] // 2
    tokens = chips * tokens_local
    me = lax.axis_index("replica")
    chip = me // 2
    core = lax.rem(me, 2)
    partner = chip * 2 + 1 - core

    def peer(chip_index):
        return {"replica": lax.rem(chip_index + chips, chips) * 2 + core}

    w_own = pltpu.make_async_copy(w_hbm, w_buf.at[core], local_sem.at[0])
    st_own = pltpu.make_async_copy(st_hbm, st_buf.at[core], local_sem.at[1])
    st_own.start()
    w_own.start()

    barrier = pltpu.get_barrier_semaphore()
    pl.semaphore_signal(barrier, inc=1, device_id={"replica": partner}, device_id_type=MESH)
    for o in range(1, chips):
        pl.semaphore_signal(barrier, inc=1, device_id=peer(chip + o), device_id_type=MESH)

    for kind, ref in enumerate((q_ref, k_ref, v_ref, g_ref)):
        for r in range(rows_local):
            at = kind * tokens_local + r * steps
            stage[at:at + steps, :] = ref[r].astype(F32)
    for o in range(chips):
        off = pl.multiple_of(lax.rem(chip + o, chips) * wide, wide)
        block = stage[:, pl.ds(off, wide)].astype(BF16)
        if o == 0:
            rbuf[0] = block
        else:
            sbuf[o] = block

    pl.semaphore_wait(barrier, chips)

    x_copies = []
    for o in range(1, chips):
        copy = pltpu.make_async_remote_copy(
            src_ref=sbuf.at[o], dst_ref=rbuf.at[o], send_sem=x_send.at[o], recv_sem=x_recv.at[o],
            device_id=peer(chip + o), device_id_type=MESH,
        )
        copy.start()
        x_copies.append(copy)
    st_pair = pltpu.make_async_remote_copy(
        src_ref=st_hbm, dst_ref=st_buf.at[core], send_sem=pair_send.at[0], recv_sem=pair_recv.at[0],
        device_id={"replica": partner}, device_id_type=MESH,
    )
    st_pair.start()
    w_pair = pltpu.make_async_remote_copy(
        src_ref=w_hbm, dst_ref=w_buf.at[core], send_sem=pair_send.at[1], recv_sem=pair_recv.at[1],
        device_id={"replica": partner}, device_id_type=MESH,
    )
    w_pair.start()

    token = lax.broadcasted_iota(jnp.int32, (tokens, 1), 0)
    source = lax.rem(chip - token // tokens_local + chips, chips)
    row = (source * 2 + core) * rows_local + lax.rem(token, tokens_local) // steps
    step = lax.rem(token, steps)
    lead_time = (step + 1).astype(F32)
    ti = lax.broadcasted_iota(jnp.int32, (tokens, tokens), 0)
    si = lax.broadcasted_iota(jnp.int32, (tokens, tokens), 1)
    live = (ti // steps == si // steps) & (si <= ti)
    gap = jnp.maximum(ti - si, 0).astype(F32)
    masks = []
    start = jnp.int32(0)
    for p in range(prompts):
        end = start + gs_ref[p]
        masks.append((row >= start) & (row < end))
        start = end

    st_own.wait()
    st_pair.wait()
    for copy in x_copies:
        copy.wait()

    us = []
    square = jnp.zeros((tokens, 1), F32)
    for h in range(2 * heads_device):
        head = chip * 2 * heads_device + h
        cols = slice(h * hd, (h + 1) * hd)
        block = rbuf[:, :, cols].astype(F32)
        q, k, v, g = (
            block[:, i * tokens_local:(i + 1) * tokens_local, :].reshape(tokens, hd) for i in range(4)
        )
        decay = decay_ref[head]
        read = jnp.zeros((tokens, hd), F32)
        keys_at = (h % heads_device) * hd
        for p in range(prompts):
            state = st_buf[h // heads_device, p, keys_at:keys_at + hd, :]
            read += jnp.dot(
                jnp.where(masks[p], q, 0.0).astype(BF16), state, preferred_element_type=F32
            )
        scores = lax.dot_general(
            q.astype(BF16), k.astype(BF16), (((1,), (1,)), ((), ())), preferred_element_type=F32
        )
        scores = scores * jnp.where(live, jnp.exp(-gap * decay), 0.0)
        high = scores.astype(BF16)
        low = (scores - high.astype(F32)).astype(BF16)
        vb = v.astype(BF16)
        recent = jnp.dot(high, vb, preferred_element_type=F32) + jnp.dot(
            low, vb, preferred_element_type=F32
        )
        attention = jnp.exp(-lead_time * decay) * read + recent
        square += jnp.sum(attention * attention, axis=1, keepdims=True)
        gain = gain_ref[pl.ds(head, 1), :]
        us.append((attention * gain * jax.nn.sigmoid(g)).astype(BF16))

    ss_send[...] = jnp.broadcast_to(square, (tokens, 128)).reshape(chips, tokens_local, 128)
    s_copies = []
    for o in range(1, chips):
        copy = pltpu.make_async_remote_copy(
            src_ref=ss_send.at[o], dst_ref=ss_recv.at[o], send_sem=s_send.at[o], recv_sem=s_recv.at[o],
            device_id=peer(chip - o), device_id_type=MESH,
        )
        copy.start()
        s_copies.append(copy)

    u0 = jnp.concatenate(us[:heads_device], axis=1)
    u1 = jnp.concatenate(us[heads_device:], axis=1)
    w_own.wait()
    w_pair.wait()
    parts, tile = pbuf.shape[0], pbuf.shape[3]
    p_copies = []
    for c in range(parts):
        pieces = []
        for base in (0, half):
            at = slice(base + c * tile, base + (c + 1) * tile)
            y = jnp.dot(u0, w_buf[0, :, at], preferred_element_type=F32)
            y += jnp.dot(u1, w_buf[1, :, at], preferred_element_type=F32)
            pieces.append(y.reshape(chips, tokens_local, tile))
        both = jnp.concatenate(pieces, axis=1)
        own[c] = both[0]
        pbuf[c] = both.astype(BF16)
        for o in range(1, chips):
            copy = pltpu.make_async_remote_copy(
                src_ref=pbuf.at[c, o], dst_ref=precv.at[c, o],
                send_sem=p_send.at[c, o], recv_sem=p_recv.at[c, o],
                device_id=peer(chip - o), device_id_type=MESH,
            )
            copy.start()
            p_copies.append(copy)

    for copy in s_copies:
        copy.wait()
    total_square = ss_send[0]
    for o in range(1, chips):
        total_square += ss_recv[o]
    scale = lax.rsqrt(total_square / features + 1e-06)[:, 0:1]
    for c in range(parts):
        total = own[c]
        for o in range(1, chips):
            p_copies[c * (chips - 1) + o - 1].wait()
            total += precv[c, o].astype(F32)
        for i, base in enumerate((0, half)):
            result = total[i * tokens_local:(i + 1) * tokens_local, :] * scale
            at = slice(base + c * tile, base + (c + 1) * tile)
            for r in range(rows_local):
                out_ref[r, :, at] = result[r * steps:(r + 1) * steps, :].astype(BF16)


def fused(
    queries, keys, values, gate_input, decay_rate, norm_gain, out_weight, prompt_states, group_sizes
):
    chips = lax.axis_size("replica") // 2
    rows_local, steps, features = queries.shape
    prompts, share, hd = prompt_states.shape
    width = out_weight.shape[1]
    tokens_local = rows_local * steps
    parts = 2
    tile = width // 2 // parts
    vmem = pl.BlockSpec(memory_space=pltpu.VMEM)
    smem = pl.BlockSpec(memory_space=pltpu.SMEM)
    hbm = pl.BlockSpec(memory_space=pl.ANY)
    dma = pltpu.SemaphoreType.DMA
    return pl.pallas_call(
        functools.partial(kernel, chips),
        out_shape=jax.ShapeDtypeStruct((rows_local, steps, width), BF16),
        in_specs=[vmem, vmem, vmem, vmem, smem, vmem, hbm, hbm, smem],
        out_specs=vmem,
        scratch_shapes=[
            pltpu.VMEM((4 * tokens_local, features), F32),
            pltpu.VMEM((chips, 4 * tokens_local, 2 * share), BF16),
            pltpu.VMEM((chips, 4 * tokens_local, 2 * share), BF16),
            pltpu.VMEM((2, share, width), BF16),
            pltpu.VMEM((2, prompts, share, hd), BF16),
            pltpu.VMEM((parts, chips, 2 * tokens_local, tile), BF16),
            pltpu.VMEM((parts, chips, 2 * tokens_local, tile), BF16),
            pltpu.VMEM((parts, 2 * tokens_local, tile), F32),
            pltpu.VMEM((chips, tokens_local, 128), F32),
            pltpu.VMEM((chips, tokens_local, 128), F32),
            dma((2,)), dma((2,)), dma((2,)),
            dma((chips,)), dma((chips,)),
            dma((parts, chips)), dma((parts, chips)),
            dma((chips,)), dma((chips,)),
        ],
        compiler_params=pltpu.CompilerParams(
            collective_id=0, has_side_effects=True, vmem_limit_bytes=48 * 1024 * 1024
        ),
    )(
        queries, keys, values, gate_input, decay_rate, norm_gain.reshape(-1, hd),
        out_weight, prompt_states, group_sizes,
    )


def general(
    queries, keys, values, gate_input, decay_rate, norm_gain, out_weight, prompt_states, group_sizes
):
    replicas = lax.axis_size("replica")
    rows_local, steps_count, features = queries.shape
    head_size = prompt_states.shape[2]
    head_count = features // head_size
    share = prompt_states.shape[1]
    rows_total = rows_local * replicas
    prompts = group_sizes.shape[0]
    order = jnp.arange(prompts)
    ends = jnp.sum(jnp.where(order[:, None] >= order[None, :], group_sizes[None, :], 0), axis=1)
    row_ids = jnp.arange(rows_total, dtype=jnp.int32)
    owners = jnp.sum((row_ids[:, None] >= ends[None, :]).astype(jnp.int32), axis=1)
    q_four = queries.reshape(rows_local, steps_count, head_count, head_size)
    k_four = keys.reshape(rows_local, steps_count, head_count, head_size)
    v_four = values.astype(F32).reshape(rows_local, steps_count, head_count, head_size)
    piece = min(share, head_size)
    pieces_here = share // piece
    per_head = head_size // piece
    query_parts = queries.reshape(rows_local, steps_count, replicas, share)
    held_queries = lax.all_to_all(query_parts, "replica", split_axis=2, concat_axis=0, tiled=True)
    held_queries = held_queries.reshape(rows_total, steps_count, pieces_here, piece)
    held_states = prompt_states.reshape(prompts, pieces_here, piece, head_size)

    def add_prompt(p, so_far):
        state = lax.dynamic_index_in_dim(held_states, p, 0, keepdims=False)
        mine = jnp.where((owners == p)[:, None, None, None], held_queries, 0)
        return so_far + jnp.einsum("rtcd,cde->rtce", mine, state, preferred_element_type=F32)

    partial_value = lax.fori_loop(
        0, prompts, add_prompt, jnp.zeros((rows_total, steps_count, pieces_here, head_size), F32)
    )
    partial_value = partial_value.reshape(replicas, rows_local, steps_count, pieces_here, head_size)
    returned = lax.all_to_all(partial_value, "replica", split_axis=0, concat_axis=0, tiled=True)
    returned = jnp.moveaxis(returned, 0, 2)
    returned = returned.reshape(rows_local, steps_count, head_count, per_head, head_size)
    prompt_read = jnp.sum(returned, axis=3)
    times = jnp.arange(1, steps_count + 1).astype(F32)
    lead = jnp.exp(-times[:, None] * decay_rate[None, :])
    gap = times[:, None] - times[None, :]
    weights_mix = jnp.where(
        gap[None] >= 0.0, jnp.exp(-jnp.maximum(gap, 0.0)[None] * decay_rate[:, None, None]), 0.0
    )
    scores = jnp.einsum("rthd,rshd->rhts", q_four, k_four, preferred_element_type=F32)
    recent = jnp.einsum(
        "rhts,rshe->rthe", scores * weights_mix[None], v_four, precision=lax.Precision.HIGHEST
    )
    attention = lead[None, :, :, None] * prompt_read + recent
    attention = attention.reshape(rows_local, steps_count, features)
    mean_square = jnp.mean(attention * attention, axis=-1, keepdims=True)
    gate = jax.nn.sigmoid(gate_input.astype(F32))
    hidden = (attention * lax.rsqrt(mean_square + 1e-06) * norm_gain * gate).astype(BF16)
    hidden = hidden.reshape(rows_local * steps_count, features)
    columns_held = lax.all_to_all(hidden, "replica", split_axis=1, concat_axis=0, tiled=True)
    sums = jnp.dot(columns_held, out_weight, preferred_element_type=F32)
    sums = sums.reshape(replicas, rows_local * steps_count, out_weight.shape[1])
    sums = lax.all_to_all(sums, "replica", split_axis=0, concat_axis=0, tiled=True)
    mixed = jnp.sum(sums, axis=0)
    return mixed.astype(BF16).reshape(rows_local, steps_count, out_weight.shape[1])


def on_device(*args):
    prompt_states = args[7]
    if prompt_states.shape[1] % prompt_states.shape[2] == 0:
        return fused(*args)
    return general(*args)


def solution(mesh):
    rows = P(("groups", "replica"), None, None)
    in_specs = (
        rows, rows, rows, rows, P(), P(), P("replica", None), P("groups", "replica", None), P("groups"),
    )
    return jax.shard_map(
        on_device, mesh=mesh, in_specs=in_specs, out_specs=rows, check_vma=False
    )
```

```python
import functools

import jax
import jax.numpy as jnp
from jax import lax
from jax.experimental import pallas as pl
from jax.experimental.pallas import tpu as pltpu
from jax.sharding import PartitionSpec as P

MESH = pl.DeviceIdType.MESH
F32 = jnp.float32
BF16 = jnp.bfloat16


def kernel(
    chips,
    q_hbm, k_hbm, v_hbm, g_hbm, decay_hbm, gain_hbm, w_hbm, st_hbm, gs_hbm,
    out_hbm,
    q_ref, k_ref, v_ref, g_ref, decay_ref, gain_ref, gs_ref, out_ref, stage, sbuf, rbuf, w_buf, st_buf, pbuf, precv, own, ss_send, ss_recv,
    local_sem, pair_send, pair_recv, x_send, x_recv, p_send, p_recv, s_send, s_recv,
):
    rows_local, steps, features = q_ref.shape
    tokens_local = rows_local * steps
    prompts, share, hd = st_hbm.shape
    wide = 2 * share
    heads_device = share // hd
    half = w_hbm.shape[1] // 2
    tokens = chips * tokens_local
    me = lax.axis_index("replica")
    chip = me // 2
    core = lax.rem(me, 2)
    partner = chip * 2 + 1 - core

    def peer(chip_index):
        return {"replica": lax.rem(chip_index + chips, chips) * 2 + core}

    w_own = pltpu.make_async_copy(w_hbm, w_buf.at[core], local_sem.at[0])
    st_own = pltpu.make_async_copy(st_hbm, st_buf.at[core], local_sem.at[1])
    loads = [
        pltpu.make_async_copy(src, dst, local_sem.at[2 + i])
        for i, (src, dst) in enumerate((
            (q_hbm, q_ref), (k_hbm, k_ref), (v_hbm, v_ref), (g_hbm, g_ref),
            (decay_hbm, decay_ref), (gs_hbm, gs_ref), (gain_hbm, gain_ref),
        ))
    ]
    for load in loads:
        load.start()
    st_own.start()
    w_own.start()

    barrier = pltpu.get_barrier_semaphore()
    pl.semaphore_signal(barrier, inc=1, device_id={"replica": partner}, device_id_type=MESH)
    for o in range(1, chips):
        pl.semaphore_signal(barrier, inc=1, device_id=peer(chip + o), device_id_type=MESH)

    for kind, ref in enumerate((q_ref, k_ref, v_ref, g_ref)):
        loads[kind].wait()
        for r in range(rows_local):
            at = kind * tokens_local + r * steps
            stage[at:at + steps, :] = ref[r].astype(F32)
    for o in range(chips):
        off = pl.multiple_of(lax.rem(chip + o, chips) * wide, wide)
        block = stage[:, pl.ds(off, wide)].astype(BF16)
        if o == 0:
            rbuf[0] = block
        else:
            sbuf[o] = block

    pl.semaphore_wait(barrier, chips)

    x_copies = []
    for o in range(1, chips):
        copy = pltpu.make_async_remote_copy(
            src_ref=sbuf.at[o], dst_ref=rbuf.at[o], send_sem=x_send.at[o], recv_sem=x_recv.at[o],
            device_id=peer(chip + o), device_id_type=MESH,
        )
        copy.start()
        x_copies.append(copy)
    st_pair = pltpu.make_async_remote_copy(
        src_ref=st_hbm, dst_ref=st_buf.at[core], send_sem=pair_send.at[0], recv_sem=pair_recv.at[0],
        device_id={"replica": partner}, device_id_type=MESH,
    )
    st_pair.start()
    w_pair = pltpu.make_async_remote_copy(
        src_ref=w_hbm, dst_ref=w_buf.at[core], send_sem=pair_send.at[1], recv_sem=pair_recv.at[1],
        device_id={"replica": partner}, device_id_type=MESH,
    )
    w_pair.start()

    token = lax.broadcasted_iota(jnp.int32, (tokens, 1), 0)
    source = lax.rem(chip - token // tokens_local + chips, chips)
    row = (source * 2 + core) * rows_local + lax.rem(token, tokens_local) // steps
    step = lax.rem(token, steps)
    lead_time = (step + 1).astype(F32)
    ti = lax.broadcasted_iota(jnp.int32, (tokens, tokens), 0)
    si = lax.broadcasted_iota(jnp.int32, (tokens, tokens), 1)
    live = (ti // steps == si // steps) & (si <= ti)
    gap = jnp.maximum(ti - si, 0).astype(F32)
    for load in loads[4:]:
        load.wait()
    masks = []
    start = jnp.int32(0)
    for p in range(prompts):
        end = start + gs_ref[p]
        masks.append((row >= start) & (row < end))
        start = end

    st_own.wait()
    st_pair.wait()
    for copy in x_copies:
        copy.wait()

    us = []
    square = jnp.zeros((tokens, 1), F32)
    for h in range(2 * heads_device):
        head = chip * 2 * heads_device + h
        cols = slice(h * hd, (h + 1) * hd)
        block = rbuf[:, :, cols].astype(F32)
        q, k, v, g = (
            block[:, i * tokens_local:(i + 1) * tokens_local, :].reshape(tokens, hd) for i in range(4)
        )
        decay = decay_ref[head]
        read = jnp.zeros((tokens, hd), F32)
        keys_at = (h % heads_device) * hd
        for p in range(prompts):
            state = st_buf[h // heads_device, p, keys_at:keys_at + hd, :]
            read += jnp.dot(
                jnp.where(masks[p], q, 0.0).astype(BF16), state, preferred_element_type=F32
            )
        scores = lax.dot_general(
            q.astype(BF16), k.astype(BF16), (((1,), (1,)), ((), ())), preferred_element_type=F32
        )
        scores = scores * jnp.where(live, jnp.exp(-gap * decay), 0.0)
        high = scores.astype(BF16)
        low = (scores - high.astype(F32)).astype(BF16)
        vb = v.astype(BF16)
        recent = jnp.dot(high, vb, preferred_element_type=F32) + jnp.dot(
            low, vb, preferred_element_type=F32
        )
        attention = jnp.exp(-lead_time * decay) * read + recent
        square += jnp.sum(attention * attention, axis=1, keepdims=True)
        gain = gain_ref[pl.ds(head, 1), :]
        us.append((attention * gain * jax.nn.sigmoid(g)).astype(BF16))

    ss_send[...] = jnp.broadcast_to(square, (tokens, 128)).reshape(chips, tokens_local, 128)
    s_copies = []
    for o in range(1, chips):
        copy = pltpu.make_async_remote_copy(
            src_ref=ss_send.at[o], dst_ref=ss_recv.at[o], send_sem=s_send.at[o], recv_sem=s_recv.at[o],
            device_id=peer(chip - o), device_id_type=MESH,
        )
        copy.start()
        s_copies.append(copy)

    u0 = jnp.concatenate(us[:heads_device], axis=1)
    u1 = jnp.concatenate(us[heads_device:], axis=1)
    w_own.wait()
    w_pair.wait()
    parts, tile = pbuf.shape[0], pbuf.shape[3]
    p_copies = []
    for c in range(parts):
        pieces = []
        for base in (0, half):
            at = slice(base + c * tile, base + (c + 1) * tile)
            y = jnp.dot(u0, w_buf[0, :, at], preferred_element_type=F32)
            y += jnp.dot(u1, w_buf[1, :, at], preferred_element_type=F32)
            pieces.append(y.reshape(chips, tokens_local, tile))
        both = jnp.concatenate(pieces, axis=1)
        own[c] = both[0]
        pbuf[c] = both.astype(BF16)
        for o in range(1, chips):
            copy = pltpu.make_async_remote_copy(
                src_ref=pbuf.at[c, o], dst_ref=precv.at[c, o],
                send_sem=p_send.at[c, o], recv_sem=p_recv.at[c, o],
                device_id=peer(chip - o), device_id_type=MESH,
            )
            copy.start()
            p_copies.append(copy)

    for copy in s_copies:
        copy.wait()
    total_square = ss_send[0]
    for o in range(1, chips):
        total_square += ss_recv[o]
    scale = lax.rsqrt(total_square / features + 1e-06)[:, 0:1]
    for c in range(parts):
        total = own[c]
        for o in range(1, chips):
            p_copies[c * (chips - 1) + o - 1].wait()
            total += precv[c, o].astype(F32)
        for i, base in enumerate((0, half)):
            result = total[i * tokens_local:(i + 1) * tokens_local, :] * scale
            at = slice(base + c * tile, base + (c + 1) * tile)
            for r in range(rows_local):
                out_ref[r, :, at] = result[r * steps:(r + 1) * steps, :].astype(BF16)
    stored = pltpu.make_async_copy(out_ref, out_hbm, local_sem.at[0])
    stored.start()
    stored.wait()


def fused(
    queries, keys, values, gate_input, decay_rate, norm_gain, out_weight, prompt_states, group_sizes
):
    chips = lax.axis_size("replica") // 2
    rows_local, steps, features = queries.shape
    prompts, share, hd = prompt_states.shape
    width = out_weight.shape[1]
    tokens_local = rows_local * steps
    parts = 2
    tile = width // 2 // parts
    hbm = pl.BlockSpec(memory_space=pl.ANY)
    dma = pltpu.SemaphoreType.DMA
    return pl.pallas_call(
        functools.partial(kernel, chips),
        out_shape=jax.ShapeDtypeStruct((rows_local, steps, width), BF16),
        in_specs=[hbm] * 9,
        out_specs=hbm,
        scratch_shapes=[
            *[pltpu.VMEM(queries.shape, BF16)] * 4,
            pltpu.SMEM(decay_rate.shape, F32),
            pltpu.VMEM((features // hd, hd), F32),
            pltpu.SMEM(group_sizes.shape, jnp.int32),
            pltpu.VMEM((rows_local, steps, width), BF16),
            pltpu.VMEM((4 * tokens_local, features), F32),
            pltpu.VMEM((chips, 4 * tokens_local, 2 * share), BF16),
            pltpu.VMEM((chips, 4 * tokens_local, 2 * share), BF16),
            pltpu.VMEM((2, share, width), BF16),
            pltpu.VMEM((2, prompts, share, hd), BF16),
            pltpu.VMEM((parts, chips, 2 * tokens_local, tile), BF16),
            pltpu.VMEM((parts, chips, 2 * tokens_local, tile), BF16),
            pltpu.VMEM((parts, 2 * tokens_local, tile), F32),
            pltpu.VMEM((chips, tokens_local, 128), F32),
            pltpu.VMEM((chips, tokens_local, 128), F32),
            dma((9,)), dma((2,)), dma((2,)),
            dma((chips,)), dma((chips,)),
            dma((parts, chips)), dma((parts, chips)),
            dma((chips,)), dma((chips,)),
        ],
        compiler_params=pltpu.CompilerParams(
            collective_id=0, has_side_effects=True, vmem_limit_bytes=60 * 1024 * 1024
        ),
    )(
        queries, keys, values, gate_input, decay_rate, norm_gain.reshape(-1, hd),
        out_weight, prompt_states, group_sizes,
    )


def general(
    queries, keys, values, gate_input, decay_rate, norm_gain, out_weight, prompt_states, group_sizes
):
    replicas = lax.axis_size("replica")
    rows_local, steps_count, features = queries.shape
    head_size = prompt_states.shape[2]
    head_count = features // head_size
    share = prompt_states.shape[1]
    rows_total = rows_local * replicas
    prompts = group_sizes.shape[0]
    order = jnp.arange(prompts)
    ends = jnp.sum(jnp.where(order[:, None] >= order[None, :], group_sizes[None, :], 0), axis=1)
    row_ids = jnp.arange(rows_total, dtype=jnp.int32)
    owners = jnp.sum((row_ids[:, None] >= ends[None, :]).astype(jnp.int32), axis=1)
    q_four = queries.reshape(rows_local, steps_count, head_count, head_size)
    k_four = keys.reshape(rows_local, steps_count, head_count, head_size)
    v_four = values.astype(F32).reshape(rows_local, steps_count, head_count, head_size)
    piece = min(share, head_size)
    pieces_here = share // piece
    per_head = head_size // piece
    query_parts = queries.reshape(rows_local, steps_count, replicas, share)
    held_queries = lax.all_to_all(query_parts, "replica", split_axis=2, concat_axis=0, tiled=True)
    held_queries = held_queries.reshape(rows_total, steps_count, pieces_here, piece)
    held_states = prompt_states.reshape(prompts, pieces_here, piece, head_size)

    def add_prompt(p, so_far):
        state = lax.dynamic_index_in_dim(held_states, p, 0, keepdims=False)
        mine = jnp.where((owners == p)[:, None, None, None], held_queries, 0)
        return so_far + jnp.einsum("rtcd,cde->rtce", mine, state, preferred_element_type=F32)

    partial_value = lax.fori_loop(
        0, prompts, add_prompt, jnp.zeros((rows_total, steps_count, pieces_here, head_size), F32)
    )
    partial_value = partial_value.reshape(replicas, rows_local, steps_count, pieces_here, head_size)
    returned = lax.all_to_all(partial_value, "replica", split_axis=0, concat_axis=0, tiled=True)
    returned = jnp.moveaxis(returned, 0, 2)
    returned = returned.reshape(rows_local, steps_count, head_count, per_head, head_size)
    prompt_read = jnp.sum(returned, axis=3)
    times = jnp.arange(1, steps_count + 1).astype(F32)
    lead = jnp.exp(-times[:, None] * decay_rate[None, :])
    gap = times[:, None] - times[None, :]
    weights_mix = jnp.where(
        gap[None] >= 0.0, jnp.exp(-jnp.maximum(gap, 0.0)[None] * decay_rate[:, None, None]), 0.0
    )
    scores = jnp.einsum("rthd,rshd->rhts", q_four, k_four, preferred_element_type=F32)
    recent = jnp.einsum(
        "rhts,rshe->rthe", scores * weights_mix[None], v_four, precision=lax.Precision.HIGHEST
    )
    attention = lead[None, :, :, None] * prompt_read + recent
    attention = attention.reshape(rows_local, steps_count, features)
    mean_square = jnp.mean(attention * attention, axis=-1, keepdims=True)
    gate = jax.nn.sigmoid(gate_input.astype(F32))
    hidden = (attention * lax.rsqrt(mean_square + 1e-06) * norm_gain * gate).astype(BF16)
    hidden = hidden.reshape(rows_local * steps_count, features)
    columns_held = lax.all_to_all(hidden, "replica", split_axis=1, concat_axis=0, tiled=True)
    sums = jnp.dot(columns_held, out_weight, preferred_element_type=F32)
    sums = sums.reshape(replicas, rows_local * steps_count, out_weight.shape[1])
    sums = lax.all_to_all(sums, "replica", split_axis=0, concat_axis=0, tiled=True)
    mixed = jnp.sum(sums, axis=0)
    return mixed.astype(BF16).reshape(rows_local, steps_count, out_weight.shape[1])


def on_device(*args):
    prompt_states = args[7]
    if prompt_states.shape[1] % prompt_states.shape[2] == 0:
        return fused(*args)
    return general(*args)


def solution(mesh):
    rows = P(("groups", "replica"), None, None)
    in_specs = (
        rows, rows, rows, rows, P(), P(), P("replica", None), P("groups", "replica", None), P("groups"),
    )
    return jax.shard_map(
        on_device, mesh=mesh, in_specs=in_specs, out_specs=rows, check_vma=False
    )
```

```python
import functools

import jax
import jax.numpy as jnp
from jax import lax
from jax.experimental import pallas as pl
from jax.experimental.pallas import tpu as pltpu
from jax.sharding import PartitionSpec as P

MESH = pl.DeviceIdType.MESH
F32 = jnp.float32
BF16 = jnp.bfloat16


def kernel(
    chips,
    q_hbm, k_hbm, v_hbm, g_hbm, decay_hbm, gain_hbm, w_hbm, st_hbm, gs_hbm,
    out_ref,
    q_ref, k_ref, v_ref, g_ref, decay_ref, gain_ref, gs_ref, stage, sbuf, rbuf, w_buf, st_buf, pbuf, precv, own, ss_send, ss_recv,
    local_sem, pair_send, pair_recv, x_send, x_recv, p_send, p_recv, s_send, s_recv,
):
    rows_local, steps, features = q_ref.shape
    tokens_local = rows_local * steps
    prompts, share, hd = st_hbm.shape
    wide = 2 * share
    heads_device = share // hd
    half = w_hbm.shape[1] // 2
    tokens = chips * tokens_local
    me = lax.axis_index("replica")
    chip = me // 2
    core = lax.rem(me, 2)
    partner = chip * 2 + 1 - core

    def peer(chip_index):
        return {"replica": lax.rem(chip_index + chips, chips) * 2 + core}

    w_own = pltpu.make_async_copy(w_hbm, w_buf.at[core], local_sem.at[0])
    st_own = pltpu.make_async_copy(st_hbm, st_buf.at[core], local_sem.at[1])
    loads = [
        pltpu.make_async_copy(src, dst, local_sem.at[2 + i])
        for i, (src, dst) in enumerate((
            (q_hbm, q_ref), (k_hbm, k_ref), (v_hbm, v_ref), (g_hbm, g_ref),
            (decay_hbm, decay_ref), (gs_hbm, gs_ref), (gain_hbm, gain_ref),
        ))
    ]
    for load in loads:
        load.start()
    st_own.start()
    w_own.start()

    barrier = pltpu.get_barrier_semaphore()
    pl.semaphore_signal(barrier, inc=1, device_id={"replica": partner}, device_id_type=MESH)
    for o in range(1, chips):
        pl.semaphore_signal(barrier, inc=1, device_id=peer(chip + o), device_id_type=MESH)

    for kind, ref in enumerate((q_ref, k_ref, v_ref, g_ref)):
        loads[kind].wait()
        for r in range(rows_local):
            at = kind * tokens_local + r * steps
            stage[at:at + steps, :] = ref[r].astype(F32)
    for o in range(chips):
        off = pl.multiple_of(lax.rem(chip + o, chips) * wide, wide)
        block = stage[:, pl.ds(off, wide)].astype(BF16)
        if o == 0:
            rbuf[0] = block
        else:
            sbuf[o] = block

    pl.semaphore_wait(barrier, chips)

    x_copies = []
    for o in range(1, chips):
        copy = pltpu.make_async_remote_copy(
            src_ref=sbuf.at[o], dst_ref=rbuf.at[o], send_sem=x_send.at[o], recv_sem=x_recv.at[o],
            device_id=peer(chip + o), device_id_type=MESH,
        )
        copy.start()
        x_copies.append(copy)
    st_pair = pltpu.make_async_remote_copy(
        src_ref=st_hbm, dst_ref=st_buf.at[core], send_sem=pair_send.at[0], recv_sem=pair_recv.at[0],
        device_id={"replica": partner}, device_id_type=MESH,
    )
    st_pair.start()
    w_pair = pltpu.make_async_remote_copy(
        src_ref=w_hbm, dst_ref=w_buf.at[core], send_sem=pair_send.at[1], recv_sem=pair_recv.at[1],
        device_id={"replica": partner}, device_id_type=MESH,
    )
    w_pair.start()

    token = lax.broadcasted_iota(jnp.int32, (tokens, 1), 0)
    source = lax.rem(chip - token // tokens_local + chips, chips)
    row = (source * 2 + core) * rows_local + lax.rem(token, tokens_local) // steps
    step = lax.rem(token, steps)
    lead_time = (step + 1).astype(F32)
    ti = lax.broadcasted_iota(jnp.int32, (tokens, tokens), 0)
    si = lax.broadcasted_iota(jnp.int32, (tokens, tokens), 1)
    live = (ti // steps == si // steps) & (si <= ti)
    gap = jnp.maximum(ti - si, 0).astype(F32)
    for load in loads[4:]:
        load.wait()
    masks = []
    start = jnp.int32(0)
    for p in range(prompts):
        end = start + gs_ref[p]
        masks.append((row >= start) & (row < end))
        start = end

    st_own.wait()
    st_pair.wait()
    for copy in x_copies:
        copy.wait()

    us = []
    square = jnp.zeros((tokens, 1), F32)
    for h in range(2 * heads_device):
        head = chip * 2 * heads_device + h
        cols = slice(h * hd, (h + 1) * hd)
        block = rbuf[:, :, cols].astype(F32)
        q, k, v, g = (
            block[:, i * tokens_local:(i + 1) * tokens_local, :].reshape(tokens, hd) for i in range(4)
        )
        decay = decay_ref[head]
        read = jnp.zeros((tokens, hd), F32)
        keys_at = (h % heads_device) * hd
        for p in range(prompts):
            state = st_buf[h // heads_device, p, keys_at:keys_at + hd, :]
            read += jnp.dot(
                jnp.where(masks[p], q, 0.0).astype(BF16), state, preferred_element_type=F32
            )
        scores = lax.dot_general(
            q.astype(BF16), k.astype(BF16), (((1,), (1,)), ((), ())), preferred_element_type=F32
        )
        scores = scores * jnp.where(live, jnp.exp(-gap * decay), 0.0)
        high = scores.astype(BF16)
        low = (scores - high.astype(F32)).astype(BF16)
        vb = v.astype(BF16)
        recent = jnp.dot(high, vb, preferred_element_type=F32) + jnp.dot(
            low, vb, preferred_element_type=F32
        )
        attention = jnp.exp(-lead_time * decay) * read + recent
        square += jnp.sum(attention * attention, axis=1, keepdims=True)
        gain = gain_ref[pl.ds(head, 1), :]
        us.append((attention * gain * jax.nn.sigmoid(g)).astype(BF16))

    ss_send[...] = jnp.broadcast_to(square, (tokens, 128)).reshape(chips, tokens_local, 128)
    s_copies = []
    for o in range(1, chips):
        copy = pltpu.make_async_remote_copy(
            src_ref=ss_send.at[o], dst_ref=ss_recv.at[o], send_sem=s_send.at[o], recv_sem=s_recv.at[o],
            device_id=peer(chip - o), device_id_type=MESH,
        )
        copy.start()
        s_copies.append(copy)

    u0 = jnp.concatenate(us[:heads_device], axis=1)
    u1 = jnp.concatenate(us[heads_device:], axis=1)
    w_own.wait()
    w_pair.wait()
    parts, tile = pbuf.shape[0], pbuf.shape[3]
    p_copies = []
    for c in range(parts):
        pieces = []
        for base in (0, half):
            at = slice(base + c * tile, base + (c + 1) * tile)
            y = jnp.dot(u0, w_buf[0, :, at], preferred_element_type=F32)
            y += jnp.dot(u1, w_buf[1, :, at], preferred_element_type=F32)
            pieces.append(y.reshape(chips, tokens_local, tile))
        both = jnp.concatenate(pieces, axis=1)
        own[c] = both[0]
        pbuf[c] = both.astype(BF16)
        for o in range(1, chips):
            copy = pltpu.make_async_remote_copy(
                src_ref=pbuf.at[c, o], dst_ref=precv.at[c, o],
                send_sem=p_send.at[c, o], recv_sem=p_recv.at[c, o],
                device_id=peer(chip - o), device_id_type=MESH,
            )
            copy.start()
            p_copies.append(copy)

    for copy in s_copies:
        copy.wait()
    total_square = ss_send[0]
    for o in range(1, chips):
        total_square += ss_recv[o]
    scale = lax.rsqrt(total_square / features + 1e-06)[:, 0:1]
    for c in range(parts):
        total = own[c]
        for o in range(1, chips):
            p_copies[c * (chips - 1) + o - 1].wait()
            total += precv[c, o].astype(F32)
        for i, base in enumerate((0, half)):
            result = total[i * tokens_local:(i + 1) * tokens_local, :] * scale
            at = slice(base + c * tile, base + (c + 1) * tile)
            for r in range(rows_local):
                out_ref[r, :, at] = result[r * steps:(r + 1) * steps, :].astype(BF16)


def fused(
    queries, keys, values, gate_input, decay_rate, norm_gain, out_weight, prompt_states, group_sizes
):
    chips = lax.axis_size("replica") // 2
    rows_local, steps, features = queries.shape
    prompts, share, hd = prompt_states.shape
    width = out_weight.shape[1]
    tokens_local = rows_local * steps
    parts = 2
    tile = width // 2 // parts
    hbm = pl.BlockSpec(memory_space=pl.ANY)
    dma = pltpu.SemaphoreType.DMA
    return pl.pallas_call(
        functools.partial(kernel, chips),
        out_shape=jax.ShapeDtypeStruct((rows_local, steps, width), BF16),
        in_specs=[hbm] * 9,
        out_specs=pl.BlockSpec(memory_space=pltpu.VMEM),
        scratch_shapes=[
            *[pltpu.VMEM(queries.shape, BF16)] * 4,
            pltpu.SMEM(decay_rate.shape, F32),
            pltpu.VMEM((features // hd, hd), F32),
            pltpu.SMEM(group_sizes.shape, jnp.int32),
            pltpu.VMEM((4 * tokens_local, features), F32),
            pltpu.VMEM((chips, 4 * tokens_local, 2 * share), BF16),
            pltpu.VMEM((chips, 4 * tokens_local, 2 * share), BF16),
            pltpu.VMEM((2, share, width), BF16),
            pltpu.VMEM((2, prompts, share, hd), BF16),
            pltpu.VMEM((parts, chips, 2 * tokens_local, tile), BF16),
            pltpu.VMEM((parts, chips, 2 * tokens_local, tile), BF16),
            pltpu.VMEM((parts, 2 * tokens_local, tile), F32),
            pltpu.VMEM((chips, tokens_local, 128), F32),
            pltpu.VMEM((chips, tokens_local, 128), F32),
            dma((9,)), dma((2,)), dma((2,)),
            dma((chips,)), dma((chips,)),
            dma((parts, chips)), dma((parts, chips)),
            dma((chips,)), dma((chips,)),
        ],
        compiler_params=pltpu.CompilerParams(
            collective_id=0, has_side_effects=True, vmem_limit_bytes=60 * 1024 * 1024
        ),
    )(
        queries, keys, values, gate_input, decay_rate, norm_gain.reshape(-1, hd),
        out_weight, prompt_states, group_sizes,
    )


def general(
    queries, keys, values, gate_input, decay_rate, norm_gain, out_weight, prompt_states, group_sizes
):
    replicas = lax.axis_size("replica")
    rows_local, steps_count, features = queries.shape
    head_size = prompt_states.shape[2]
    head_count = features // head_size
    share = prompt_states.shape[1]
    rows_total = rows_local * replicas
    prompts = group_sizes.shape[0]
    order = jnp.arange(prompts)
    ends = jnp.sum(jnp.where(order[:, None] >= order[None, :], group_sizes[None, :], 0), axis=1)
    row_ids = jnp.arange(rows_total, dtype=jnp.int32)
    owners = jnp.sum((row_ids[:, None] >= ends[None, :]).astype(jnp.int32), axis=1)
    q_four = queries.reshape(rows_local, steps_count, head_count, head_size)
    k_four = keys.reshape(rows_local, steps_count, head_count, head_size)
    v_four = values.astype(F32).reshape(rows_local, steps_count, head_count, head_size)
    piece = min(share, head_size)
    pieces_here = share // piece
    per_head = head_size // piece
    query_parts = queries.reshape(rows_local, steps_count, replicas, share)
    held_queries = lax.all_to_all(query_parts, "replica", split_axis=2, concat_axis=0, tiled=True)
    held_queries = held_queries.reshape(rows_total, steps_count, pieces_here, piece)
    held_states = prompt_states.reshape(prompts, pieces_here, piece, head_size)

    def add_prompt(p, so_far):
        state = lax.dynamic_index_in_dim(held_states, p, 0, keepdims=False)
        mine = jnp.where((owners == p)[:, None, None, None], held_queries, 0)
        return so_far + jnp.einsum("rtcd,cde->rtce", mine, state, preferred_element_type=F32)

    partial_value = lax.fori_loop(
        0, prompts, add_prompt, jnp.zeros((rows_total, steps_count, pieces_here, head_size), F32)
    )
    partial_value = partial_value.reshape(replicas, rows_local, steps_count, pieces_here, head_size)
    returned = lax.all_to_all(partial_value, "replica", split_axis=0, concat_axis=0, tiled=True)
    returned = jnp.moveaxis(returned, 0, 2)
    returned = returned.reshape(rows_local, steps_count, head_count, per_head, head_size)
    prompt_read = jnp.sum(returned, axis=3)
    times = jnp.arange(1, steps_count + 1).astype(F32)
    lead = jnp.exp(-times[:, None] * decay_rate[None, :])
    gap = times[:, None] - times[None, :]
    weights_mix = jnp.where(
        gap[None] >= 0.0, jnp.exp(-jnp.maximum(gap, 0.0)[None] * decay_rate[:, None, None]), 0.0
    )
    scores = jnp.einsum("rthd,rshd->rhts", q_four, k_four, preferred_element_type=F32)
    recent = jnp.einsum(
        "rhts,rshe->rthe", scores * weights_mix[None], v_four, precision=lax.Precision.HIGHEST
    )
    attention = lead[None, :, :, None] * prompt_read + recent
    attention = attention.reshape(rows_local, steps_count, features)
    mean_square = jnp.mean(attention * attention, axis=-1, keepdims=True)
    gate = jax.nn.sigmoid(gate_input.astype(F32))
    hidden = (attention * lax.rsqrt(mean_square + 1e-06) * norm_gain * gate).astype(BF16)
    hidden = hidden.reshape(rows_local * steps_count, features)
    columns_held = lax.all_to_all(hidden, "replica", split_axis=1, concat_axis=0, tiled=True)
    sums = jnp.dot(columns_held, out_weight, preferred_element_type=F32)
    sums = sums.reshape(replicas, rows_local * steps_count, out_weight.shape[1])
    sums = lax.all_to_all(sums, "replica", split_axis=0, concat_axis=0, tiled=True)
    mixed = jnp.sum(sums, axis=0)
    return mixed.astype(BF16).reshape(rows_local, steps_count, out_weight.shape[1])


def on_device(*args):
    prompt_states = args[7]
    if prompt_states.shape[1] % prompt_states.shape[2] == 0:
        return fused(*args)
    return general(*args)


def solution(mesh):
    rows = P(("groups", "replica"), None, None)
    in_specs = (
        rows, rows, rows, rows, P(), P(), P("replica", None), P("groups", "replica", None), P("groups"),
    )
    return jax.shard_map(
        on_device, mesh=mesh, in_specs=in_specs, out_specs=rows, check_vma=False
    )
```

```python
import functools

import jax
import jax.numpy as jnp
from jax import lax
from jax.experimental import pallas as pl
from jax.experimental.pallas import tpu as pltpu
from jax.sharding import PartitionSpec as P

MESH = pl.DeviceIdType.MESH
F32 = jnp.float32
BF16 = jnp.bfloat16


def kernel(
    chips,
    q_hbm, k_hbm, v_hbm, g_hbm, decay_hbm, gain_hbm, w_hbm, st_hbm, gs_hbm,
    out_ref,
    q_ref, k_ref, v_ref, g_ref, decay_ref, gain_ref, gs_ref, stage, sbuf, rbuf, w_buf, st_buf, pbuf, precv, own, ss_send, ss_recv,
    local_sem, pair_send, pair_recv, x_send, x_recv, p_send, p_recv, s_send, s_recv,
):
    rows_local, steps, features = q_ref.shape
    tokens_local = rows_local * steps
    prompts, share, hd = st_hbm.shape
    wide = 2 * share
    heads_device = share // hd
    half = w_hbm.shape[1] // 2
    tokens = chips * tokens_local
    me = lax.axis_index("replica")
    chip = me // 2
    core = lax.rem(me, 2)
    partner = chip * 2 + 1 - core

    def peer(chip_index):
        return {"replica": lax.rem(chip_index + chips, chips) * 2 + core}

    w_own = pltpu.make_async_copy(w_hbm, w_buf.at[core], local_sem.at[0])
    st_own = pltpu.make_async_copy(st_hbm, st_buf.at[core], local_sem.at[1])
    loads = [
        pltpu.make_async_copy(src, dst, local_sem.at[2 + i])
        for i, (src, dst) in enumerate((
            (q_hbm, q_ref), (k_hbm, k_ref), (v_hbm, v_ref), (g_hbm, g_ref),
            (decay_hbm, decay_ref), (gs_hbm, gs_ref), (gain_hbm, gain_ref),
        ))
    ]
    for load in loads:
        load.start()
    st_own.start()
    w_own.start()

    barrier = pltpu.get_barrier_semaphore()
    pl.semaphore_signal(barrier, inc=1, device_id={"replica": partner}, device_id_type=MESH)
    for o in range(1, chips):
        pl.semaphore_signal(barrier, inc=1, device_id=peer(chip + o), device_id_type=MESH)

    for kind, ref in enumerate((q_ref, k_ref, v_ref, g_ref)):
        loads[kind].wait()
        for r in range(rows_local):
            at = kind * tokens_local + r * steps
            stage[at:at + steps, :] = ref[r].astype(F32)
    for o in range(chips):
        off = pl.multiple_of(lax.rem(chip + o, chips) * wide, wide)
        block = stage[:, pl.ds(off, wide)].astype(BF16)
        if o == 0:
            rbuf[0] = block
        else:
            sbuf[o] = block

    pl.semaphore_wait(barrier, chips)

    far_first = sorted(range(1, chips), key=lambda i: -min(i, chips - i))
    x_copies = []
    for o in far_first:
        copy = pltpu.make_async_remote_copy(
            src_ref=sbuf.at[o], dst_ref=rbuf.at[o], send_sem=x_send.at[o], recv_sem=x_recv.at[o],
            device_id=peer(chip + o), device_id_type=MESH,
        )
        copy.start()
        x_copies.append(copy)
    st_pair = pltpu.make_async_remote_copy(
        src_ref=st_hbm, dst_ref=st_buf.at[core], send_sem=pair_send.at[0], recv_sem=pair_recv.at[0],
        device_id={"replica": partner}, device_id_type=MESH,
    )
    st_pair.start()
    w_pair = pltpu.make_async_remote_copy(
        src_ref=w_hbm, dst_ref=w_buf.at[core], send_sem=pair_send.at[1], recv_sem=pair_recv.at[1],
        device_id={"replica": partner}, device_id_type=MESH,
    )
    w_pair.start()

    token = lax.broadcasted_iota(jnp.int32, (tokens, 1), 0)
    source = lax.rem(chip - token // tokens_local + chips, chips)
    row = (source * 2 + core) * rows_local + lax.rem(token, tokens_local) // steps
    step = lax.rem(token, steps)
    lead_time = (step + 1).astype(F32)
    ti = lax.broadcasted_iota(jnp.int32, (tokens, tokens), 0)
    si = lax.broadcasted_iota(jnp.int32, (tokens, tokens), 1)
    live = (ti // steps == si // steps) & (si <= ti)
    gap = jnp.maximum(ti - si, 0).astype(F32)
    for load in loads[4:]:
        load.wait()
    masks = []
    start = jnp.int32(0)
    for p in range(prompts):
        end = start + gs_ref[p]
        masks.append((row >= start) & (row < end))
        start = end

    st_own.wait()
    st_pair.wait()
    for copy in x_copies:
        copy.wait()

    us = []
    square = jnp.zeros((tokens, 1), F32)
    for h in range(2 * heads_device):
        head = chip * 2 * heads_device + h
        cols = slice(h * hd, (h + 1) * hd)
        block = rbuf[:, :, cols].astype(F32)
        q, k, v, g = (
            block[:, i * tokens_local:(i + 1) * tokens_local, :].reshape(tokens, hd) for i in range(4)
        )
        decay = decay_ref[head]
        read = jnp.zeros((tokens, hd), F32)
        keys_at = (h % heads_device) * hd
        for p in range(prompts):
            state = st_buf[h // heads_device, p, keys_at:keys_at + hd, :]
            read += jnp.dot(
                jnp.where(masks[p], q, 0.0).astype(BF16), state, preferred_element_type=F32
            )
        scores = lax.dot_general(
            q.astype(BF16), k.astype(BF16), (((1,), (1,)), ((), ())), preferred_element_type=F32
        )
        scores = scores * jnp.where(live, jnp.exp(-gap * decay), 0.0)
        high = scores.astype(BF16)
        low = (scores - high.astype(F32)).astype(BF16)
        vb = v.astype(BF16)
        recent = jnp.dot(high, vb, preferred_element_type=F32) + jnp.dot(
            low, vb, preferred_element_type=F32
        )
        attention = jnp.exp(-lead_time * decay) * read + recent
        square += jnp.sum(attention * attention, axis=1, keepdims=True)
        gain = gain_ref[pl.ds(head, 1), :]
        us.append((attention * gain * jax.nn.sigmoid(g)).astype(BF16))

    ss_send[...] = jnp.broadcast_to(square, (tokens, 128)).reshape(chips, tokens_local, 128)
    s_copies = []
    for o in range(1, chips):
        copy = pltpu.make_async_remote_copy(
            src_ref=ss_send.at[o], dst_ref=ss_recv.at[o], send_sem=s_send.at[o], recv_sem=s_recv.at[o],
            device_id=peer(chip - o), device_id_type=MESH,
        )
        copy.start()
        s_copies.append(copy)

    u0 = jnp.concatenate(us[:heads_device], axis=1)
    u1 = jnp.concatenate(us[heads_device:], axis=1)
    w_own.wait()
    w_pair.wait()
    parts, tile = pbuf.shape[0], pbuf.shape[3]
    p_copies = {}
    for c in range(parts):
        pieces = []
        for base in (0, half):
            at = slice(base + c * tile, base + (c + 1) * tile)
            y = jnp.dot(u0, w_buf[0, :, at], preferred_element_type=F32)
            y += jnp.dot(u1, w_buf[1, :, at], preferred_element_type=F32)
            pieces.append(y.reshape(chips, tokens_local, tile))
        both = jnp.concatenate(pieces, axis=1)
        own[c] = both[0]
        pbuf[c] = both.astype(BF16)
        for o in far_first:
            copy = pltpu.make_async_remote_copy(
                src_ref=pbuf.at[c, o], dst_ref=precv.at[c, o],
                send_sem=p_send.at[c, o], recv_sem=p_recv.at[c, o],
                device_id=peer(chip - o), device_id_type=MESH,
            )
            copy.start()
            p_copies[c, o] = copy

    for copy in s_copies:
        copy.wait()
    total_square = ss_send[0]
    for o in range(1, chips):
        total_square += ss_recv[o]
    scale = lax.rsqrt(total_square / features + 1e-06)[:, 0:1]
    for c in range(parts):
        total = own[c]
        for o in range(1, chips):
            p_copies[c, o].wait()
            total += precv[c, o].astype(F32)
        for i, base in enumerate((0, half)):
            result = total[i * tokens_local:(i + 1) * tokens_local, :] * scale
            at = slice(base + c * tile, base + (c + 1) * tile)
            for r in range(rows_local):
                out_ref[r, :, at] = result[r * steps:(r + 1) * steps, :].astype(BF16)


def fused(
    queries, keys, values, gate_input, decay_rate, norm_gain, out_weight, prompt_states, group_sizes
):
    chips = lax.axis_size("replica") // 2
    rows_local, steps, features = queries.shape
    prompts, share, hd = prompt_states.shape
    width = out_weight.shape[1]
    tokens_local = rows_local * steps
    parts = 2
    tile = width // 2 // parts
    hbm = pl.BlockSpec(memory_space=pl.ANY)
    dma = pltpu.SemaphoreType.DMA
    return pl.pallas_call(
        functools.partial(kernel, chips),
        out_shape=jax.ShapeDtypeStruct((rows_local, steps, width), BF16),
        in_specs=[hbm] * 9,
        out_specs=pl.BlockSpec(memory_space=pltpu.VMEM),
        scratch_shapes=[
            *[pltpu.VMEM(queries.shape, BF16)] * 4,
            pltpu.SMEM(decay_rate.shape, F32),
            pltpu.VMEM((features // hd, hd), F32),
            pltpu.SMEM(group_sizes.shape, jnp.int32),
            pltpu.VMEM((4 * tokens_local, features), F32),
            pltpu.VMEM((chips, 4 * tokens_local, 2 * share), BF16),
            pltpu.VMEM((chips, 4 * tokens_local, 2 * share), BF16),
            pltpu.VMEM((2, share, width), BF16),
            pltpu.VMEM((2, prompts, share, hd), BF16),
            pltpu.VMEM((parts, chips, 2 * tokens_local, tile), BF16),
            pltpu.VMEM((parts, chips, 2 * tokens_local, tile), BF16),
            pltpu.VMEM((parts, 2 * tokens_local, tile), F32),
            pltpu.VMEM((chips, tokens_local, 128), F32),
            pltpu.VMEM((chips, tokens_local, 128), F32),
            dma((9,)), dma((2,)), dma((2,)),
            dma((chips,)), dma((chips,)),
            dma((parts, chips)), dma((parts, chips)),
            dma((chips,)), dma((chips,)),
        ],
        compiler_params=pltpu.CompilerParams(
            collective_id=0, has_side_effects=True, vmem_limit_bytes=60 * 1024 * 1024
        ),
    )(
        queries, keys, values, gate_input, decay_rate, norm_gain.reshape(-1, hd),
        out_weight, prompt_states, group_sizes,
    )


def general(
    queries, keys, values, gate_input, decay_rate, norm_gain, out_weight, prompt_states, group_sizes
):
    replicas = lax.axis_size("replica")
    rows_local, steps_count, features = queries.shape
    head_size = prompt_states.shape[2]
    head_count = features // head_size
    share = prompt_states.shape[1]
    rows_total = rows_local * replicas
    prompts = group_sizes.shape[0]
    order = jnp.arange(prompts)
    ends = jnp.sum(jnp.where(order[:, None] >= order[None, :], group_sizes[None, :], 0), axis=1)
    row_ids = jnp.arange(rows_total, dtype=jnp.int32)
    owners = jnp.sum((row_ids[:, None] >= ends[None, :]).astype(jnp.int32), axis=1)
    q_four = queries.reshape(rows_local, steps_count, head_count, head_size)
    k_four = keys.reshape(rows_local, steps_count, head_count, head_size)
    v_four = values.astype(F32).reshape(rows_local, steps_count, head_count, head_size)
    piece = min(share, head_size)
    pieces_here = share // piece
    per_head = head_size // piece
    query_parts = queries.reshape(rows_local, steps_count, replicas, share)
    held_queries = lax.all_to_all(query_parts, "replica", split_axis=2, concat_axis=0, tiled=True)
    held_queries = held_queries.reshape(rows_total, steps_count, pieces_here, piece)
    held_states = prompt_states.reshape(prompts, pieces_here, piece, head_size)

    def add_prompt(p, so_far):
        state = lax.dynamic_index_in_dim(held_states, p, 0, keepdims=False)
        mine = jnp.where((owners == p)[:, None, None, None], held_queries, 0)
        return so_far + jnp.einsum("rtcd,cde->rtce", mine, state, preferred_element_type=F32)

    partial_value = lax.fori_loop(
        0, prompts, add_prompt, jnp.zeros((rows_total, steps_count, pieces_here, head_size), F32)
    )
    partial_value = partial_value.reshape(replicas, rows_local, steps_count, pieces_here, head_size)
    returned = lax.all_to_all(partial_value, "replica", split_axis=0, concat_axis=0, tiled=True)
    returned = jnp.moveaxis(returned, 0, 2)
    returned = returned.reshape(rows_local, steps_count, head_count, per_head, head_size)
    prompt_read = jnp.sum(returned, axis=3)
    times = jnp.arange(1, steps_count + 1).astype(F32)
    lead = jnp.exp(-times[:, None] * decay_rate[None, :])
    gap = times[:, None] - times[None, :]
    weights_mix = jnp.where(
        gap[None] >= 0.0, jnp.exp(-jnp.maximum(gap, 0.0)[None] * decay_rate[:, None, None]), 0.0
    )
    scores = jnp.einsum("rthd,rshd->rhts", q_four, k_four, preferred_element_type=F32)
    recent = jnp.einsum(
        "rhts,rshe->rthe", scores * weights_mix[None], v_four, precision=lax.Precision.HIGHEST
    )
    attention = lead[None, :, :, None] * prompt_read + recent
    attention = attention.reshape(rows_local, steps_count, features)
    mean_square = jnp.mean(attention * attention, axis=-1, keepdims=True)
    gate = jax.nn.sigmoid(gate_input.astype(F32))
    hidden = (attention * lax.rsqrt(mean_square + 1e-06) * norm_gain * gate).astype(BF16)
    hidden = hidden.reshape(rows_local * steps_count, features)
    columns_held = lax.all_to_all(hidden, "replica", split_axis=1, concat_axis=0, tiled=True)
    sums = jnp.dot(columns_held, out_weight, preferred_element_type=F32)
    sums = sums.reshape(replicas, rows_local * steps_count, out_weight.shape[1])
    sums = lax.all_to_all(sums, "replica", split_axis=0, concat_axis=0, tiled=True)
    mixed = jnp.sum(sums, axis=0)
    return mixed.astype(BF16).reshape(rows_local, steps_count, out_weight.shape[1])


def on_device(*args):
    prompt_states = args[7]
    if prompt_states.shape[1] % prompt_states.shape[2] == 0:
        return fused(*args)
    return general(*args)


def solution(mesh):
    rows = P(("groups", "replica"), None, None)
    in_specs = (
        rows, rows, rows, rows, P(), P(), P("replica", None), P("groups", "replica", None), P("groups"),
    )
    return jax.shard_map(
        on_device, mesh=mesh, in_specs=in_specs, out_specs=rows, check_vma=False
    )
```

```python
import functools

import jax
import jax.numpy as jnp
from jax import lax
from jax.experimental import pallas as pl
from jax.experimental.pallas import tpu as pltpu
from jax.sharding import PartitionSpec as P

MESH = pl.DeviceIdType.MESH
F32 = jnp.float32
BF16 = jnp.bfloat16


def kernel(
    chips,
    q_hbm, k_hbm, v_hbm, g_hbm, decay_hbm, gain_hbm, w_hbm, st_hbm, gs_hbm,
    out_ref,
    q_ref, k_ref, v_ref, g_ref, decay_ref, gain_ref, gs_ref, stage, sbuf, rbuf, w_buf, st_buf, sums, side_send, side_recv, pbuf, precv, own, ss_send, ss_recv,
    local_sem, pair_send, pair_recv, x_send, x_recv, p_send, p_recv, s_send, s_recv, c_send, c_recv,
):
    rows_local, steps, features = q_ref.shape
    tokens_local = rows_local * steps
    prompts, share, hd = st_hbm.shape
    wide = 2 * share
    heads_device = share // hd
    half = w_hbm.shape[1] // 2
    tokens = chips * tokens_local
    me = lax.axis_index("replica")
    chip = me // 2
    core = lax.rem(me, 2)
    partner = chip * 2 + 1 - core

    def peer(chip_index):
        return {"replica": lax.rem(chip_index + chips, chips) * 2 + core}

    w_own = pltpu.make_async_copy(w_hbm, w_buf.at[core], local_sem.at[0])
    st_own = pltpu.make_async_copy(st_hbm, st_buf.at[core], local_sem.at[1])
    loads = [
        pltpu.make_async_copy(src, dst, local_sem.at[2 + i])
        for i, (src, dst) in enumerate((
            (q_hbm, q_ref), (k_hbm, k_ref), (v_hbm, v_ref), (g_hbm, g_ref),
            (decay_hbm, decay_ref), (gs_hbm, gs_ref), (gain_hbm, gain_ref),
        ))
    ]
    for load in loads:
        load.start()
    st_own.start()
    w_own.start()

    barrier = pltpu.get_barrier_semaphore()
    pl.semaphore_signal(barrier, inc=1, device_id={"replica": partner}, device_id_type=MESH)
    for o in range(1, chips):
        pl.semaphore_signal(barrier, inc=1, device_id=peer(chip + o), device_id_type=MESH)

    for kind, ref in enumerate((q_ref, k_ref, v_ref, g_ref)):
        loads[kind].wait()
        for r in range(rows_local):
            at = kind * tokens_local + r * steps
            stage[at:at + steps, :] = ref[r].astype(F32)
    for o in range(chips):
        off = pl.multiple_of(lax.rem(chip + o, chips) * wide, wide)
        block = stage[:, pl.ds(off, wide)].astype(BF16)
        if o == 0:
            rbuf[0] = block
        else:
            sbuf[o] = block

    pl.semaphore_wait(barrier, chips)

    far_first = sorted(range(1, chips), key=lambda i: -min(i, chips - i))
    x_copies = []
    for o in far_first:
        copy = pltpu.make_async_remote_copy(
            src_ref=sbuf.at[o], dst_ref=rbuf.at[o], send_sem=x_send.at[o], recv_sem=x_recv.at[o],
            device_id=peer(chip + o), device_id_type=MESH,
        )
        copy.start()
        x_copies.append(copy)
    st_pair = pltpu.make_async_remote_copy(
        src_ref=st_hbm, dst_ref=st_buf.at[core], send_sem=pair_send.at[0], recv_sem=pair_recv.at[0],
        device_id={"replica": partner}, device_id_type=MESH,
    )
    st_pair.start()
    w_pair = pltpu.make_async_remote_copy(
        src_ref=w_hbm, dst_ref=w_buf.at[core], send_sem=pair_send.at[1], recv_sem=pair_recv.at[1],
        device_id={"replica": partner}, device_id_type=MESH,
    )
    w_pair.start()

    token = lax.broadcasted_iota(jnp.int32, (tokens, 1), 0)
    source = lax.rem(chip - token // tokens_local + chips, chips)
    row = (source * 2 + core) * rows_local + lax.rem(token, tokens_local) // steps
    step = lax.rem(token, steps)
    lead_time = (step + 1).astype(F32)
    ti = lax.broadcasted_iota(jnp.int32, (tokens, tokens), 0)
    si = lax.broadcasted_iota(jnp.int32, (tokens, tokens), 1)
    live = (ti // steps == si // steps) & (si <= ti)
    gap = jnp.maximum(ti - si, 0).astype(F32)
    for load in loads[4:]:
        load.wait()
    masks = []
    start = jnp.int32(0)
    for p in range(prompts):
        end = start + gs_ref[p]
        masks.append((row >= start) & (row < end))
        start = end

    st_own.wait()
    st_pair.wait()
    for copy in x_copies:
        copy.wait()

    us = []
    square = jnp.zeros((tokens, 1), F32)
    for h in range(2 * heads_device):
        head = chip * 2 * heads_device + h
        cols = slice(h * hd, (h + 1) * hd)
        block = rbuf[:, :, cols].astype(F32)
        q, k, v, g = (
            block[:, i * tokens_local:(i + 1) * tokens_local, :].reshape(tokens, hd) for i in range(4)
        )
        decay = decay_ref[head]
        read = jnp.zeros((tokens, hd), F32)
        keys_at = (h % heads_device) * hd
        for p in range(prompts):
            state = st_buf[h // heads_device, p, keys_at:keys_at + hd, :]
            read += jnp.dot(
                jnp.where(masks[p], q, 0.0).astype(BF16), state, preferred_element_type=F32
            )
        scores = lax.dot_general(
            q.astype(BF16), k.astype(BF16), (((1,), (1,)), ((), ())), preferred_element_type=F32
        )
        scores = scores * jnp.where(live, jnp.exp(-gap * decay), 0.0)
        high = scores.astype(BF16)
        low = (scores - high.astype(F32)).astype(BF16)
        vb = v.astype(BF16)
        recent = jnp.dot(high, vb, preferred_element_type=F32) + jnp.dot(
            low, vb, preferred_element_type=F32
        )
        attention = jnp.exp(-lead_time * decay) * read + recent
        square += jnp.sum(attention * attention, axis=1, keepdims=True)
        gain = gain_ref[pl.ds(head, 1), :]
        us.append((attention * gain * jax.nn.sigmoid(g)).astype(BF16))

    ss_send[...] = jnp.broadcast_to(square, (tokens, 128)).reshape(chips, tokens_local, 128)
    s_copies = []
    for o in range(1, chips):
        copy = pltpu.make_async_remote_copy(
            src_ref=ss_send.at[o], dst_ref=ss_recv.at[o], send_sem=s_send.at[o], recv_sem=s_recv.at[o],
            device_id=peer(chip - o), device_id_type=MESH,
        )
        copy.start()
        s_copies.append(copy)

    u0 = jnp.concatenate(us[:heads_device], axis=1)
    u1 = jnp.concatenate(us[heads_device:], axis=1)
    w_own.wait()
    w_pair.wait()
    parts, _, _, tile = sums.shape
    lines = chips // 2
    parity = lax.rem(chip, 2)
    side_copies = []
    for c in range(parts):
        pieces = []
        for base in (0, half):
            at = slice(base + c * tile, base + (c + 1) * tile)
            y = jnp.dot(u0, w_buf[0, :, at], preferred_element_type=F32)
            y += jnp.dot(u1, w_buf[1, :, at], preferred_element_type=F32)
            pieces.append(y.reshape(chips, tokens_local, tile))
        both = jnp.concatenate(pieces, axis=1)
        for m in range(lines):
            sums[c, m] = both[2 * m]
            side_send[c, m] = both[2 * m + 1].astype(BF16)
        copy = pltpu.make_async_remote_copy(
            src_ref=side_send.at[c], dst_ref=side_recv.at[c],
            send_sem=c_send.at[c], recv_sem=c_recv.at[c],
            device_id=peer(chip + 1 - 2 * parity), device_id_type=MESH,
        )
        copy.start()
        side_copies.append(copy)

    line_first = sorted(range(1, lines), key=lambda i: -min(i, lines - i))
    p_copies = {}
    for c in range(parts):
        side_copies[c].wait()
        for m in line_first + [0]:
            total = sums[c, m] + side_recv[c, lax.rem(m + lines - parity, lines)].astype(F32)
            if m == 0:
                own[c] = total
                continue
            pbuf[c, m] = total.astype(BF16)
            copy = pltpu.make_async_remote_copy(
                src_ref=pbuf.at[c, m], dst_ref=precv.at[c, m],
                send_sem=p_send.at[c, m], recv_sem=p_recv.at[c, m],
                device_id=peer(chip - 2 * m), device_id_type=MESH,
            )
            copy.start()
            p_copies[c, m] = copy

    for copy in s_copies:
        copy.wait()
    total_square = ss_send[0]
    for o in range(1, chips):
        total_square += ss_recv[o]
    scale = lax.rsqrt(total_square / features + 1e-06)[:, 0:1]
    for c in range(parts):
        total = own[c]
        for m in range(1, lines):
            p_copies[c, m].wait()
            total += precv[c, m].astype(F32)
        for i, base in enumerate((0, half)):
            result = total[i * tokens_local:(i + 1) * tokens_local, :] * scale
            at = slice(base + c * tile, base + (c + 1) * tile)
            for r in range(rows_local):
                out_ref[r, :, at] = result[r * steps:(r + 1) * steps, :].astype(BF16)


def fused(
    queries, keys, values, gate_input, decay_rate, norm_gain, out_weight, prompt_states, group_sizes
):
    chips = lax.axis_size("replica") // 2
    rows_local, steps, features = queries.shape
    prompts, share, hd = prompt_states.shape
    width = out_weight.shape[1]
    tokens_local = rows_local * steps
    parts = 4
    tile = width // 2 // parts
    hbm = pl.BlockSpec(memory_space=pl.ANY)
    dma = pltpu.SemaphoreType.DMA
    return pl.pallas_call(
        functools.partial(kernel, chips),
        out_shape=jax.ShapeDtypeStruct((rows_local, steps, width), BF16),
        in_specs=[hbm] * 9,
        out_specs=pl.BlockSpec(memory_space=pltpu.VMEM),
        scratch_shapes=[
            *[pltpu.VMEM(queries.shape, BF16)] * 4,
            pltpu.SMEM(decay_rate.shape, F32),
            pltpu.VMEM((features // hd, hd), F32),
            pltpu.SMEM(group_sizes.shape, jnp.int32),
            pltpu.VMEM((4 * tokens_local, features), F32),
            pltpu.VMEM((chips, 4 * tokens_local, 2 * share), BF16),
            pltpu.VMEM((chips, 4 * tokens_local, 2 * share), BF16),
            pltpu.VMEM((2, share, width), BF16),
            pltpu.VMEM((2, prompts, share, hd), BF16),
            pltpu.VMEM((parts, chips // 2, 2 * tokens_local, tile), F32),
            pltpu.VMEM((parts, chips // 2, 2 * tokens_local, tile), BF16),
            pltpu.VMEM((parts, chips // 2, 2 * tokens_local, tile), BF16),
            pltpu.VMEM((parts, chips // 2, 2 * tokens_local, tile), BF16),
            pltpu.VMEM((parts, chips // 2, 2 * tokens_local, tile), BF16),
            pltpu.VMEM((parts, 2 * tokens_local, tile), F32),
            pltpu.VMEM((chips, tokens_local, 128), F32),
            pltpu.VMEM((chips, tokens_local, 128), F32),
            dma((9,)), dma((2,)), dma((2,)),
            dma((chips,)), dma((chips,)),
            dma((parts, chips // 2)), dma((parts, chips // 2)),
            dma((chips,)), dma((chips,)), dma((parts,)), dma((parts,)),
        ],
        compiler_params=pltpu.CompilerParams(
            collective_id=0, has_side_effects=True, vmem_limit_bytes=60 * 1024 * 1024
        ),
    )(
        queries, keys, values, gate_input, decay_rate, norm_gain.reshape(-1, hd),
        out_weight, prompt_states, group_sizes,
    )


def general(
    queries, keys, values, gate_input, decay_rate, norm_gain, out_weight, prompt_states, group_sizes
):
    replicas = lax.axis_size("replica")
    rows_local, steps_count, features = queries.shape
    head_size = prompt_states.shape[2]
    head_count = features // head_size
    share = prompt_states.shape[1]
    rows_total = rows_local * replicas
    prompts = group_sizes.shape[0]
    order = jnp.arange(prompts)
    ends = jnp.sum(jnp.where(order[:, None] >= order[None, :], group_sizes[None, :], 0), axis=1)
    row_ids = jnp.arange(rows_total, dtype=jnp.int32)
    owners = jnp.sum((row_ids[:, None] >= ends[None, :]).astype(jnp.int32), axis=1)
    q_four = queries.reshape(rows_local, steps_count, head_count, head_size)
    k_four = keys.reshape(rows_local, steps_count, head_count, head_size)
    v_four = values.astype(F32).reshape(rows_local, steps_count, head_count, head_size)
    piece = min(share, head_size)
    pieces_here = share // piece
    per_head = head_size // piece
    query_parts = queries.reshape(rows_local, steps_count, replicas, share)
    held_queries = lax.all_to_all(query_parts, "replica", split_axis=2, concat_axis=0, tiled=True)
    held_queries = held_queries.reshape(rows_total, steps_count, pieces_here, piece)
    held_states = prompt_states.reshape(prompts, pieces_here, piece, head_size)

    def add_prompt(p, so_far):
        state = lax.dynamic_index_in_dim(held_states, p, 0, keepdims=False)
        mine = jnp.where((owners == p)[:, None, None, None], held_queries, 0)
        return so_far + jnp.einsum("rtcd,cde->rtce", mine, state, preferred_element_type=F32)

    partial_value = lax.fori_loop(
        0, prompts, add_prompt, jnp.zeros((rows_total, steps_count, pieces_here, head_size), F32)
    )
    partial_value = partial_value.reshape(replicas, rows_local, steps_count, pieces_here, head_size)
    returned = lax.all_to_all(partial_value, "replica", split_axis=0, concat_axis=0, tiled=True)
    returned = jnp.moveaxis(returned, 0, 2)
    returned = returned.reshape(rows_local, steps_count, head_count, per_head, head_size)
    prompt_read = jnp.sum(returned, axis=3)
    times = jnp.arange(1, steps_count + 1).astype(F32)
    lead = jnp.exp(-times[:, None] * decay_rate[None, :])
    gap = times[:, None] - times[None, :]
    weights_mix = jnp.where(
        gap[None] >= 0.0, jnp.exp(-jnp.maximum(gap, 0.0)[None] * decay_rate[:, None, None]), 0.0
    )
    scores = jnp.einsum("rthd,rshd->rhts", q_four, k_four, preferred_element_type=F32)
    recent = jnp.einsum(
        "rhts,rshe->rthe", scores * weights_mix[None], v_four, precision=lax.Precision.HIGHEST
    )
    attention = lead[None, :, :, None] * prompt_read + recent
    attention = attention.reshape(rows_local, steps_count, features)
    mean_square = jnp.mean(attention * attention, axis=-1, keepdims=True)
    gate = jax.nn.sigmoid(gate_input.astype(F32))
    hidden = (attention * lax.rsqrt(mean_square + 1e-06) * norm_gain * gate).astype(BF16)
    hidden = hidden.reshape(rows_local * steps_count, features)
    columns_held = lax.all_to_all(hidden, "replica", split_axis=1, concat_axis=0, tiled=True)
    sums = jnp.dot(columns_held, out_weight, preferred_element_type=F32)
    sums = sums.reshape(replicas, rows_local * steps_count, out_weight.shape[1])
    sums = lax.all_to_all(sums, "replica", split_axis=0, concat_axis=0, tiled=True)
    mixed = jnp.sum(sums, axis=0)
    return mixed.astype(BF16).reshape(rows_local, steps_count, out_weight.shape[1])


def on_device(*args):
    prompt_states = args[7]
    aligned = prompt_states.shape[1] % prompt_states.shape[2] == 0
    if aligned and lax.axis_size("replica") % 4 == 0:
        return fused(*args)
    return general(*args)


def solution(mesh):
    rows = P(("groups", "replica"), None, None)
    in_specs = (
        rows, rows, rows, rows, P(), P(), P("replica", None), P("groups", "replica", None), P("groups"),
    )
    return jax.shard_map(
        on_device, mesh=mesh, in_specs=in_specs, out_specs=rows, check_vma=False
    )
```

```python
import functools

import jax
import jax.numpy as jnp
from jax import lax
from jax.experimental import pallas as pl
from jax.experimental.pallas import tpu as pltpu
from jax.sharding import PartitionSpec as P

MESH = pl.DeviceIdType.MESH
F32 = jnp.float32
BF16 = jnp.bfloat16


def kernel(
    chips,
    q_hbm, k_hbm, v_hbm, g_hbm, decay_hbm, gain_hbm, w_hbm, st_hbm, gs_hbm,
    out_ref,
    q_ref, k_ref, v_ref, g_ref, decay_ref, gain_ref, gs_ref, stage, sbuf, rbuf, w_buf, st_buf, pbuf, precv, own, ss_send, ss_recv,
    local_sem, pair_send, pair_recv, x_send, x_recv, p_send, p_recv, s_send, s_recv,
):
    rows_local, steps, features = q_ref.shape
    tokens_local = rows_local * steps
    prompts, share, hd = st_hbm.shape
    wide = 2 * share
    heads_device = share // hd
    half = w_hbm.shape[1] // 2
    tokens = chips * tokens_local
    me = lax.axis_index("replica")
    chip = me // 2
    core = lax.rem(me, 2)
    partner = chip * 2 + 1 - core

    def peer(chip_index):
        return {"replica": lax.rem(chip_index + chips, chips) * 2 + core}

    barrier = pltpu.get_barrier_semaphore()
    far_first = sorted(range(1, chips), key=lambda i: -min(i, chips - i))
    for o in far_first:
        pl.semaphore_signal(barrier, inc=1, device_id=peer(chip + o), device_id_type=MESH)
    pl.semaphore_signal(barrier, inc=1, device_id={"replica": partner}, device_id_type=MESH)

    w_own = pltpu.make_async_copy(w_hbm, w_buf.at[core], local_sem.at[0])
    st_own = pltpu.make_async_copy(st_hbm, st_buf.at[core], local_sem.at[1])
    loads = [
        pltpu.make_async_copy(src, dst, local_sem.at[2 + i])
        for i, (src, dst) in enumerate((
            (q_hbm, q_ref), (k_hbm, k_ref), (v_hbm, v_ref), (g_hbm, g_ref),
            (decay_hbm, decay_ref), (gs_hbm, gs_ref), (gain_hbm, gain_ref),
        ))
    ]
    for load in loads:
        load.start()
    st_own.start()
    w_own.start()

    for kind, ref in enumerate((q_ref, k_ref, v_ref, g_ref)):
        loads[kind].wait()
        for r in range(rows_local):
            at = kind * tokens_local + r * steps
            stage[at:at + steps, :] = ref[r].astype(F32)
    for o in range(chips):
        off = pl.multiple_of(lax.rem(chip + o, chips) * wide, wide)
        block = stage[:, pl.ds(off, wide)].astype(BF16)
        if o == 0:
            rbuf[0] = block
        else:
            sbuf[o] = block

    pl.semaphore_wait(barrier, chips)

    x_copies = []
    for o in far_first:
        copy = pltpu.make_async_remote_copy(
            src_ref=sbuf.at[o], dst_ref=rbuf.at[o], send_sem=x_send.at[o], recv_sem=x_recv.at[o],
            device_id=peer(chip + o), device_id_type=MESH,
        )
        copy.start()
        x_copies.append(copy)
    st_pair = pltpu.make_async_remote_copy(
        src_ref=st_hbm, dst_ref=st_buf.at[core], send_sem=pair_send.at[0], recv_sem=pair_recv.at[0],
        device_id={"replica": partner}, device_id_type=MESH,
    )
    st_pair.start()
    w_pair = pltpu.make_async_remote_copy(
        src_ref=w_hbm, dst_ref=w_buf.at[core], send_sem=pair_send.at[1], recv_sem=pair_recv.at[1],
        device_id={"replica": partner}, device_id_type=MESH,
    )
    w_pair.start()

    token = lax.broadcasted_iota(jnp.int32, (tokens, 1), 0)
    source = lax.rem(chip - token // tokens_local + chips, chips)
    row = (source * 2 + core) * rows_local + lax.rem(token, tokens_local) // steps
    step = lax.rem(token, steps)
    lead_time = (step + 1).astype(F32)
    ti = lax.broadcasted_iota(jnp.int32, (tokens, tokens), 0)
    si = lax.broadcasted_iota(jnp.int32, (tokens, tokens), 1)
    live = (ti // steps == si // steps) & (si <= ti)
    gap = jnp.maximum(ti - si, 0).astype(F32)
    for load in loads[4:]:
        load.wait()
    masks = []
    start = jnp.int32(0)
    for p in range(prompts):
        end = start + gs_ref[p]
        masks.append((row >= start) & (row < end))
        start = end

    st_own.wait()
    st_pair.wait()
    for copy in x_copies:
        copy.wait()

    us = []
    square = jnp.zeros((tokens, 1), F32)
    for h in range(2 * heads_device):
        head = chip * 2 * heads_device + h
        cols = slice(h * hd, (h + 1) * hd)
        block = rbuf[:, :, cols].astype(F32)
        q, k, v, g = (
            block[:, i * tokens_local:(i + 1) * tokens_local, :].reshape(tokens, hd) for i in range(4)
        )
        decay = decay_ref[head]
        read = jnp.zeros((tokens, hd), F32)
        keys_at = (h % heads_device) * hd
        for p in range(prompts):
            state = st_buf[h // heads_device, p, keys_at:keys_at + hd, :]
            read += jnp.dot(
                jnp.where(masks[p], q, 0.0).astype(BF16), state, preferred_element_type=F32
            )
        scores = lax.dot_general(
            q.astype(BF16), k.astype(BF16), (((1,), (1,)), ((), ())), preferred_element_type=F32
        )
        scores = scores * jnp.where(live, jnp.exp(-gap * decay), 0.0)
        high = scores.astype(BF16)
        low = (scores - high.astype(F32)).astype(BF16)
        vb = v.astype(BF16)
        recent = jnp.dot(high, vb, preferred_element_type=F32) + jnp.dot(
            low, vb, preferred_element_type=F32
        )
        attention = jnp.exp(-lead_time * decay) * read + recent
        square += jnp.sum(attention * attention, axis=1, keepdims=True)
        gain = gain_ref[pl.ds(head, 1), :]
        us.append((attention * gain * jax.nn.sigmoid(g)).astype(BF16))

    ss_send[...] = jnp.broadcast_to(square, (tokens, 128)).reshape(chips, tokens_local, 128)
    s_copies = []
    for o in range(1, chips):
        copy = pltpu.make_async_remote_copy(
            src_ref=ss_send.at[o], dst_ref=ss_recv.at[o], send_sem=s_send.at[o], recv_sem=s_recv.at[o],
            device_id=peer(chip - o), device_id_type=MESH,
        )
        copy.start()
        s_copies.append(copy)

    u0 = jnp.concatenate(us[:heads_device], axis=1)
    u1 = jnp.concatenate(us[heads_device:], axis=1)
    w_own.wait()
    w_pair.wait()
    parts, tile = pbuf.shape[0], pbuf.shape[3]
    p_copies = {}
    for c in range(parts):
        pieces = []
        for base in (0, half):
            at = slice(base + c * tile, base + (c + 1) * tile)
            y = jnp.dot(u0, w_buf[0, :, at], preferred_element_type=F32)
            y += jnp.dot(u1, w_buf[1, :, at], preferred_element_type=F32)
            pieces.append(y.reshape(chips, tokens_local, tile))
        both = jnp.concatenate(pieces, axis=1)
        own[c] = both[0]
        pbuf[c] = both.astype(BF16)
        for o in far_first:
            copy = pltpu.make_async_remote_copy(
                src_ref=pbuf.at[c, o], dst_ref=precv.at[c, o],
                send_sem=p_send.at[c, o], recv_sem=p_recv.at[c, o],
                device_id=peer(chip - o), device_id_type=MESH,
            )
            copy.start()
            p_copies[c, o] = copy

    for copy in s_copies:
        copy.wait()
    total_square = ss_send[0]
    for o in range(1, chips):
        total_square += ss_recv[o]
    scale = lax.rsqrt(total_square / features + 1e-06)[:, 0:1]
    for c in range(parts):
        total = own[c]
        for o in range(1, chips):
            p_copies[c, o].wait()
            total += precv[c, o].astype(F32)
        for i, base in enumerate((0, half)):
            result = total[i * tokens_local:(i + 1) * tokens_local, :] * scale
            at = slice(base + c * tile, base + (c + 1) * tile)
            for r in range(rows_local):
                out_ref[r, :, at] = result[r * steps:(r + 1) * steps, :].astype(BF16)


def fused(
    queries, keys, values, gate_input, decay_rate, norm_gain, out_weight, prompt_states, group_sizes
):
    chips = lax.axis_size("replica") // 2
    rows_local, steps, features = queries.shape
    prompts, share, hd = prompt_states.shape
    width = out_weight.shape[1]
    tokens_local = rows_local * steps
    parts = 2
    tile = width // 2 // parts
    hbm = pl.BlockSpec(memory_space=pl.ANY)
    dma = pltpu.SemaphoreType.DMA
    return pl.pallas_call(
        functools.partial(kernel, chips),
        out_shape=jax.ShapeDtypeStruct((rows_local, steps, width), BF16),
        in_specs=[hbm] * 9,
        out_specs=pl.BlockSpec(memory_space=pltpu.VMEM),
        scratch_shapes=[
            *[pltpu.VMEM(queries.shape, BF16)] * 4,
            pltpu.SMEM(decay_rate.shape, F32),
            pltpu.VMEM((features // hd, hd), F32),
            pltpu.SMEM(group_sizes.shape, jnp.int32),
            pltpu.VMEM((4 * tokens_local, features), F32),
            pltpu.VMEM((chips, 4 * tokens_local, 2 * share), BF16),
            pltpu.VMEM((chips, 4 * tokens_local, 2 * share), BF16),
            pltpu.VMEM((2, share, width), BF16),
            pltpu.VMEM((2, prompts, share, hd), BF16),
            pltpu.VMEM((parts, chips, 2 * tokens_local, tile), BF16),
            pltpu.VMEM((parts, chips, 2 * tokens_local, tile), BF16),
            pltpu.VMEM((parts, 2 * tokens_local, tile), F32),
            pltpu.VMEM((chips, tokens_local, 128), F32),
            pltpu.VMEM((chips, tokens_local, 128), F32),
            dma((9,)), dma((2,)), dma((2,)),
            dma((chips,)), dma((chips,)),
            dma((parts, chips)), dma((parts, chips)),
            dma((chips,)), dma((chips,)),
        ],
        compiler_params=pltpu.CompilerParams(
            collective_id=0, has_side_effects=True, vmem_limit_bytes=60 * 1024 * 1024
        ),
    )(
        queries, keys, values, gate_input, decay_rate, norm_gain.reshape(-1, hd),
        out_weight, prompt_states, group_sizes,
    )


def general(
    queries, keys, values, gate_input, decay_rate, norm_gain, out_weight, prompt_states, group_sizes
):
    replicas = lax.axis_size("replica")
    rows_local, steps_count, features = queries.shape
    head_size = prompt_states.shape[2]
    head_count = features // head_size
    share = prompt_states.shape[1]
    rows_total = rows_local * replicas
    prompts = group_sizes.shape[0]
    order = jnp.arange(prompts)
    ends = jnp.sum(jnp.where(order[:, None] >= order[None, :], group_sizes[None, :], 0), axis=1)
    row_ids = jnp.arange(rows_total, dtype=jnp.int32)
    owners = jnp.sum((row_ids[:, None] >= ends[None, :]).astype(jnp.int32), axis=1)
    q_four = queries.reshape(rows_local, steps_count, head_count, head_size)
    k_four = keys.reshape(rows_local, steps_count, head_count, head_size)
    v_four = values.astype(F32).reshape(rows_local, steps_count, head_count, head_size)
    piece = min(share, head_size)
    pieces_here = share // piece
    per_head = head_size // piece
    query_parts = queries.reshape(rows_local, steps_count, replicas, share)
    held_queries = lax.all_to_all(query_parts, "replica", split_axis=2, concat_axis=0, tiled=True)
    held_queries = held_queries.reshape(rows_total, steps_count, pieces_here, piece)
    held_states = prompt_states.reshape(prompts, pieces_here, piece, head_size)

    def add_prompt(p, so_far):
        state = lax.dynamic_index_in_dim(held_states, p, 0, keepdims=False)
        mine = jnp.where((owners == p)[:, None, None, None], held_queries, 0)
        return so_far + jnp.einsum("rtcd,cde->rtce", mine, state, preferred_element_type=F32)

    partial_value = lax.fori_loop(
        0, prompts, add_prompt, jnp.zeros((rows_total, steps_count, pieces_here, head_size), F32)
    )
    partial_value = partial_value.reshape(replicas, rows_local, steps_count, pieces_here, head_size)
    returned = lax.all_to_all(partial_value, "replica", split_axis=0, concat_axis=0, tiled=True)
    returned = jnp.moveaxis(returned, 0, 2)
    returned = returned.reshape(rows_local, steps_count, head_count, per_head, head_size)
    prompt_read = jnp.sum(returned, axis=3)
    times = jnp.arange(1, steps_count + 1).astype(F32)
    lead = jnp.exp(-times[:, None] * decay_rate[None, :])
    gap = times[:, None] - times[None, :]
    weights_mix = jnp.where(
        gap[None] >= 0.0, jnp.exp(-jnp.maximum(gap, 0.0)[None] * decay_rate[:, None, None]), 0.0
    )
    scores = jnp.einsum("rthd,rshd->rhts", q_four, k_four, preferred_element_type=F32)
    recent = jnp.einsum(
        "rhts,rshe->rthe", scores * weights_mix[None], v_four, precision=lax.Precision.HIGHEST
    )
    attention = lead[None, :, :, None] * prompt_read + recent
    attention = attention.reshape(rows_local, steps_count, features)
    mean_square = jnp.mean(attention * attention, axis=-1, keepdims=True)
    gate = jax.nn.sigmoid(gate_input.astype(F32))
    hidden = (attention * lax.rsqrt(mean_square + 1e-06) * norm_gain * gate).astype(BF16)
    hidden = hidden.reshape(rows_local * steps_count, features)
    columns_held = lax.all_to_all(hidden, "replica", split_axis=1, concat_axis=0, tiled=True)
    sums = jnp.dot(columns_held, out_weight, preferred_element_type=F32)
    sums = sums.reshape(replicas, rows_local * steps_count, out_weight.shape[1])
    sums = lax.all_to_all(sums, "replica", split_axis=0, concat_axis=0, tiled=True)
    mixed = jnp.sum(sums, axis=0)
    return mixed.astype(BF16).reshape(rows_local, steps_count, out_weight.shape[1])


def on_device(*args):
    prompt_states = args[7]
    if prompt_states.shape[1] % prompt_states.shape[2] == 0:
        return fused(*args)
    return general(*args)


def solution(mesh):
    rows = P(("groups", "replica"), None, None)
    in_specs = (
        rows, rows, rows, rows, P(), P(), P("replica", None), P("groups", "replica", None), P("groups"),
    )
    return jax.shard_map(
        on_device, mesh=mesh, in_specs=in_specs, out_specs=rows, check_vma=False
    )
```
